32 devices in a mesh: tm: 4 (over z), dp: 8 (over y, x, core).
Axes of the slice: x: 2, y: 2, z: 4, core: 2. Of those that a mesh axis runs over, the one named last changes fastest.
Arguments:
- clip_video: bfloat16 [8, 8, 4, 16, 192], P('dp', 'tm'), may hold values from -6 to 6
- clip_ids: int32 [8, 8], P('dp'), may hold values from 0 to 3, never falling along the last dimension, each value on 1 to 4 neighbouring positions
- norm_gain: float32 [192], replicated, may hold values from 0.25 to 1.75
- conv_weight: bfloat16 [5184, 384], replicated, may hold values from -0.078125 to 0.078125
- out_cotangent: bfloat16 [8, 8, 4, 16, 384], P('dp', 'tm'), may hold values from -6 to 6
Outputs:
- conv_out: bfloat16 [8, 8, 4, 16, 384], P('dp', 'tm')
- grad_video: bfloat16 [8, 8, 4, 16, 192], P('dp', 'tm')
- grad_weight: float32 [5184, 384], P('tm', 'dp')
The draws below stay inside these ranges and needn't reach their ends.
Inputs may be any that keep to these rules, and one draw needn't show every extreme that they name: `clip_ids`: within each group clip numbers never fall along the frames; each clip lasts 1 to 4 frames and one lasts exactly 4.
All inputs are finite; a program needn't handle non-finite values.
Results may differ from the reference program's by a relative error of at most 0.0049.
Values may be sent and summed in bfloat16 or wider, within the bound.
A program may use at most 64 MiB of HBM per device.

```python
import math
import jax
import jax.numpy as jnp
import numpy as np
from jax import lax

C_IN = 192
C_OUT = 384
H = 4
W = 16
KROWS = 5184
FRAMES = 8
GROUPS = 8


def with_spikes(result, own_key, source, target, shards_of, factor):
    owner, partner = [(jnp.arange(result.shape[position]) // (result.shape[position] // shards_of)).reshape([-1 if axis == position else 1 for axis in range(result.ndim)]) for position in (source, target)]
    chosen = jax.random.permutation(own_key, shards_of)[partner]
    strong = (owner == chosen) | (owner == (partner + shards_of // 2) % shards_of)
    return jnp.where(strong, factor * result, result)


def block_scale(key, extent, pieces, low, largest):
    def one(position, parts):
        heights = jax.random.uniform(jax.random.fold_in(jax.random.fold_in(key, 6), position), (parts,), jnp.float32, low / len(pieces), largest / len(pieces))
        return jnp.repeat(jnp.exp(heights), extent[position] // parts).reshape((-1,) + (1,) * (len(extent) - position - 1))

    loudness = one(*pieces[0])
    for cut in pieces[1:]:
        loudness = loudness * one(*cut)
    return loudness


def split_up(number_of, total, reach, slope):
    portions = [(1 << 20) // math.isqrt(standing ** slope) + 1 for standing in range(2, number_of + 1)]
    spare, counts = total - reach - (number_of - 1), [1] * (number_of - 1)
    while spare > 0:
        movable = [i for i in range(number_of - 1) if counts[i] < reach]
        whole, left = sum([portions[i] for i in movable]), spare
        for i in movable:
            more = min(reach - counts[i], max(1, left * portions[i] // whole), spare)
            counts[i] = counts[i] + more
            spare = spare - more
    return np.array([reach] + counts)


def uneven(key, amount, total, limit, skew):
    if amount == 2:
        one = jax.random.randint(key, (), max(1, total - limit), min(limit, total - 1) + 1)
        return jnp.stack([one, total - one])
    lengths = jnp.asarray(split_up(amount, total, limit, skew), jnp.int32)
    pairs = (amount - 1) // 2
    giver, sink = lengths[1:1 + 2 * pairs:2], lengths[2:2 + 2 * pairs:2]
    slack = jnp.minimum(giver - 1, limit - sink)
    shifted = jax.random.randint(jax.random.fold_in(key, 1), (pairs,), 0, 1 << 20) % (slack + 1)
    lengths = lengths.at[1:1 + 2 * pairs:2].set(giver - shifted).at[2:2 + 2 * pairs:2].set(sink + shifted)
    return lengths[jax.random.permutation(jax.random.fold_in(key, 2), amount)]


def centred(key, extent, scale, most, shards=(), kind=jnp.bfloat16):
    factor_of = block_scale(key, extent, shards, -0.22, 0.18) if shards else 1.0
    values = jax.random.normal(key, extent, jnp.float32) * scale * factor_of
    return jnp.minimum(jnp.maximum(values, -most), most).astype(kind)


def heavy_noise(key, dims, deviation, reach, cuts, heavy, held_as=jnp.bfloat16):
    array = deviation * jax.random.normal(key, dims, jnp.float32)
    if cuts:
        array = array * block_scale(key, dims, cuts, -0.22, 0.18)
    return jnp.clip(with_spikes(array, jax.random.fold_in(key, 3), *heavy), -reach, reach).astype(held_as)


def setup_inputs(seed: int = 0) -> dict:
    arg_keys = jax.random.split(jax.random.key(seed), 6)
    return {
        "clip_video": centred(arg_keys[0], (GROUPS, FRAMES, H, W, C_IN), 1.0, 6.0, ((0, 8), (1, 4))),
        "clip_ids": jax.vmap(lambda own: jnp.searchsorted(jnp.cumsum(uneven(own, 4, FRAMES, FRAMES // 2, 1)), jnp.arange(FRAMES), side="right"))(jax.random.split(arg_keys[1], GROUPS)).reshape((GROUPS, FRAMES)).astype(jnp.int32),
        "norm_gain": jnp.clip(1.0 + 0.15 * jax.random.normal(arg_keys[2], (C_IN,), jnp.float32), 0.25, 1.75),
        "conv_weight": centred(arg_keys[3], (KROWS, C_OUT), KROWS ** -0.5, 0.078125),
        "out_cotangent": heavy_noise(arg_keys[4], (GROUPS, FRAMES, H, W, C_OUT), 1.0, 6.0, ((0, 8), (1, 4)), (0, 4, 8, 2.0)),
    }


def activate(video, norm_gain):
    values = video.astype(jnp.float32)
    mean_square = lax.optimization_barrier(jnp.mean(values * values, axis=-1, keepdims=True))
    normed = values * lax.rsqrt(mean_square + 1e-06) * norm_gain
    return jax.nn.silu(normed)

def make_mask(clips, first_frame, count):
    padded_ids = jnp.concatenate([jnp.full((2,), -1, jnp.int32), clips.astype(jnp.int32)])
    window = lax.dynamic_slice_in_dim(padded_ids, first_frame, count + 2)
    offsets = jnp.arange(count)[:, None] + jnp.arange(3)[None, :]
    current = window[jnp.arange(count) + 2][:, None]
    return (window[offsets] == current).astype(jnp.float32)

def extract(extended, tap_mask):
    frames = tap_mask.shape[0]
    height, width = (extended.shape[1], extended.shape[2])
    padded = jnp.pad(extended, ((0, 0), (1, 1), (1, 1), (0, 0)))
    taps = []
    for tap_t in range(3):
        weight_t = tap_mask[:, tap_t][:, None, None, None].astype(extended.dtype)
        for tap_h in range(3):
            for tap_w in range(3):
                taps.append(padded[tap_t:tap_t + frames, tap_h:tap_h + height, tap_w:tap_w + width] * weight_t)
    stacked = jnp.stack(taps, axis=3)
    return stacked.reshape(frames * height * width, -1)

def reference(clip_video, clip_ids, norm_gain, conv_weight, out_cotangent):
    frames, height, width, channels = clip_video.shape[1:]
    outputs = conv_weight.shape[1]

    def one_group(weight_sum, items):
        video, cotangent, clips = items
        activated = activate(video, norm_gain).astype(jnp.bfloat16)
        extended = jnp.concatenate([jnp.zeros((2, height, width, channels), jnp.bfloat16), activated])
        tap_mask = make_mask(clips, 0, frames)
        patches = extract(extended, tap_mask)
        conv_rows = jnp.dot(patches, conv_weight, preferred_element_type=jnp.float32).astype(jnp.bfloat16)
        cotangent_rows = cotangent.reshape(-1, outputs)
        weight_sum = weight_sum + jnp.dot(patches.T, cotangent_rows, preferred_element_type=jnp.float32)
        patch_grad = jnp.dot(cotangent_rows, conv_weight.T, preferred_element_type=jnp.float32)
        unused, pull_patch = jax.vjp(lambda field: extract(field, tap_mask), extended.astype(jnp.float32))
        extended_grad = pull_patch(patch_grad)[0]
        unused, pull_norm = jax.vjp(lambda field: activate(field, norm_gain), video.astype(jnp.float32))
        video_grad = pull_norm(extended_grad[2:])[0].astype(jnp.bfloat16)
        return (weight_sum, (conv_rows.reshape(frames, height, width, outputs), video_grad))
    start_sum = jnp.zeros(conv_weight.shape, jnp.float32)
    weight_sum, (conv_out, grad_video) = lax.scan(one_group, start_sum, (clip_video, out_cotangent, clip_ids))
    scale = 1.0 / math.sqrt(clip_video.shape[0] * frames * height * width)
    return (conv_out, grad_video, weight_sum * scale)
```

```python
import functools
import math

import jax
import jax.numpy as jnp
from jax import lax
from jax.experimental import pallas as pl
from jax.experimental.pallas import tpu as pltpu
from jax.sharding import PartitionSpec as P

MESH = pl.DeviceIdType.MESH
F32 = jnp.float32
BF16 = jnp.bfloat16


def half_roll(x):
    return pltpu.roll(x, 64, axis=1)


def shifted(x, width, b):
    if b == 1:
        return x
    rows = x.shape[0]
    column = lax.broadcasted_iota(jnp.int32, x.shape, 0) % width
    if b == 0:
        return jnp.where(column == 0, 0.0, pltpu.roll(x, 1, axis=0))
    return jnp.where(column == width - 1, 0.0, pltpu.roll(x, rows - 1, axis=0))


def kernel(
    cfg, video_ref, ids_ref, gain_ref, w_hbm, cot_ref, conv_ref, vgrad_ref, gw_ref,
    w_ref, pay, ext, cext, mask, cot_t, d32, d16, r1, s16, s32, r2,
    w_sem, send_r, send_l, recv_r, recv_l, core_send, core_recv, chip_send, chip_recv,
):
    tm, dp, frames, height, width, cin, cout, slab, pairs, fused = cfg
    total = tm * frames
    rows = frames * height * width
    pixels = height * width
    chunks = cout // 128
    z = lax.axis_index("tm")
    j = lax.axis_index("dp")
    core = j % 2
    chip = j // 2
    chips = dp // 2
    per = cout // dp

    w_copy = pltpu.make_async_copy(w_hbm, w_ref, w_sem)
    w_copy.start()

    barrier = pltpu.get_barrier_semaphore()

    def greet(where):
        pl.semaphore_signal(barrier, inc=1, device_id=where, device_id_type=MESH)

    @pl.when(z > 0)
    def _():
        greet((z - 1, j))

    @pl.when(z < tm - 1)
    def _():
        greet((z + 1, j))

    if fused:
        greet((z, chip * 2 + 1 - core))
        for r in range(1, chips):
            greet((z, (chip + r) % chips * 2 + core))

    video = video_ref[...].astype(F32)
    gain = gain_ref[...]
    mean_square = jnp.sum(video * video, axis=1, keepdims=True) / cin
    inv = lax.rsqrt(mean_square + 1e-06)
    normed = video * inv * gain
    sig = jax.nn.sigmoid(normed)
    act = (normed * sig).astype(BF16).astype(F32)
    lane = lax.broadcasted_iota(jnp.int32, (rows, 128), 1)
    low = lane < 64
    first = act[:, :128]
    second = jnp.concatenate([act[:, 128:], jnp.zeros((rows, 64), F32)], axis=1)
    half = rows // 2
    for m in range(chunks):
        pay[z, m * rows : (m + 1) * rows, :] = cot_ref[:, m * 128 : (m + 1) * 128]
    pay[z, chunks * rows : (chunks + 1) * rows, :] = first.astype(BF16)
    pay[z, (chunks + 1) * rows :, :] = (second[:half] + half_roll(second[half:])).astype(BF16)

    peers = jnp.where(z > 0, 1, 0) + jnp.where(z < tm - 1, 1, 0)
    if fused:
        peers = peers + chips
    pl.semaphore_wait(barrier, peers)

    def to_right(step, shard):
        return pltpu.make_async_remote_copy(
            src_ref=pay.at[shard], dst_ref=pay.at[shard], send_sem=send_r.at[step],
            recv_sem=recv_r.at[step], device_id=(z + 1, j), device_id_type=MESH,
        )

    def to_left(step, shard):
        return pltpu.make_async_remote_copy(
            src_ref=pay.at[shard], dst_ref=pay.at[shard], send_sem=send_l.at[step],
            recv_sem=recv_l.at[step], device_id=(z - 1, j), device_id_type=MESH,
        )

    def start_step(step):
        @pl.when((z < tm - 1) & (z - step >= 0))
        def _():
            to_right(step, z - step).start()

        @pl.when((z > 0) & (z + step <= tm - 1))
        def _():
            to_left(step, z + step).start()

    start_step(0)

    ext[...] = jnp.zeros(ext.shape, BF16)
    cext[...] = jnp.zeros(cext.shape, BF16)
    mask[...] = jnp.zeros(mask.shape, BF16)
    for t in range(total):
        for k in range(3):
            if t - 2 + k >= 0:
                same = jnp.where(ids_ref[0, t - 2 + k] == ids_ref[0, t], 1.0, 0.0)
                mask[k, t] = jnp.full((pixels, 128), same, F32).astype(BF16)

    def blocks(x):
        return x.astype(BF16).reshape(frames, height, width, 128)

    def place(shard):
        t0 = pay[shard, chunks * rows : (chunks + 1) * rows, :].astype(F32)
        pack = pay[shard, (chunks + 1) * rows :, :].astype(F32)
        plow = low[:half]
        t1 = jnp.concatenate(
            [jnp.where(plow, pack, 0.0), half_roll(jnp.where(plow, 0.0, pack))], axis=0
        )
        tiles = (
            (t0, t1),
            (half_roll(jnp.where(low, t0, 0.0)), half_roll(jnp.where(low, t1, t0))),
        )
        at = pl.ds(shard * frames + 2, frames)
        for b in range(3):
            for v in range(2):
                for n in range(2):
                    ext[v, b, at, 1 : 1 + height, :, n * 128 : (n + 1) * 128] = blocks(
                        shifted(tiles[v][n], width, b)
                    )
        turned = jnp.concatenate(
            [
                jnp.transpose(pay[shard, m * rows : (m + 1) * rows, :])
                for m in range(chunks)
            ],
            axis=0,
        )
        if fused:
            for d in range(chips):
                for e in range(2):
                    at_row = (e * chips + d) * per
                    from_row = (d * 2 + e) * per
                    cot_t[shard, at_row : at_row + per, :] = turned[from_row : from_row + per]
        else:
            cot_t[shard] = turned

    def place_cot(shard, frame):
        for m in range(chunks):
            tile = pay[shard, m * rows : (m + 1) * rows, :].astype(F32)
            for b in range(3):
                cext[b, frame : frame + frames, 1 : 1 + height, :, m * 128 : (m + 1) * 128] = blocks(
                    shifted(tile, width, b)
                )

    place(z)
    place_cot(z, 0)

    def finish_step(step):
        @pl.when(z - 1 - step >= 0)
        def _():
            to_right(step, z - 1 - step).wait_recv()

        @pl.when(z + 1 + step <= tm - 1)
        def _():
            to_left(step, z + 1 + step).wait_recv()

        if step + 1 < tm - 1:
            start_step(step + 1)

        @pl.when(z - 1 - step >= 0)
        def _():
            place(z - 1 - step)

        @pl.when(z + 1 + step <= tm - 1)
        def _():
            place(z + 1 + step)
            if step == 0:
                place_cot(z + 1, frames)

    def pair_tiles(one, two, at, count):
        n = count * pixels

        def part(v, tap):
            k, a, b = tap
            block = ext[v, b, pl.ds(at + k, count), pl.ds(a, height), :, :]
            scale = mask[k, pl.ds(at, count)].reshape(n, 128)
            block = block.reshape(n, 256)
            return block[:, :128] * scale, block[:, 128:] * scale

        a0, a1 = part(0, one)
        if two is None:
            return [a0, a1[:, : cin - 128]]
        b0, b1 = part(1, two)
        return [a0, a1 + b0, b1]

    def conv_some(taps):
        tiles = []
        for n in range(0, len(taps), 2):
            two = taps[n + 1] if n + 1 < len(taps) else None
            tiles += pair_tiles(split(taps[n]), None if two is None else split(two), z * frames, frames)
        return jnp.dot(
            jnp.concatenate(tiles, axis=1),
            w_ref[taps[0] * cin : (taps[-1] + 1) * cin, :],
            preferred_element_type=F32,
        )

    def split(tap):
        return tap // 9, tap // 3 % 3, tap % 3

    finish_step(0)
    w_copy.wait()
    groups = [list(range(n, min(n + 4, 27))) for n in range(0, 27, 4)]
    steps_left = max(tm - 2, 1)
    conv = jnp.zeros((rows, cout), F32)
    done = 0
    for step in range(1, tm):
        upto = len(groups) * step // steps_left if step <= steps_left else len(groups)
        while done < upto:
            conv = conv + conv_some(groups[done])
            done += 1
        if step < tm - 1:
            finish_step(step)
    conv_ref[...] = conv.astype(BF16)

    first_tap = z * slab // cin
    cot_all = jnp.concatenate([cot_t[s] for s in range(tm)], axis=1)

    def core_copy(p):
        return pltpu.make_async_remote_copy(
            src_ref=d16.at[p, 1 - core], dst_ref=r1.at[p], send_sem=core_send.at[p],
            recv_sem=core_recv.at[p], device_id=(z, chip * 2 + 1 - core), device_id_type=MESH,
        )

    def chip_copy(p, r):
        there = (chip + r) % chips
        return pltpu.make_async_remote_copy(
            src_ref=s16.at[p, there], dst_ref=r2.at[p, r - 1], send_sem=chip_send.at[p, r - 1],
            recv_sem=chip_recv.at[p, r - 1], device_id=(z, there * 2 + core), device_id_type=MESH,
        )

    def core_sum(p):
        core_copy(p).wait_recv()
        both = d32[p, core] + r1[p].astype(F32)
        both = both.reshape(chips, per, 2 * cin)
        s32[p] = both
        s16[p] = both.astype(BF16)
        for r in range(1, chips):
            chip_copy(p, r).start()

    for p in range(pairs):
        patches = jnp.concatenate(
            pair_tiles(split(first_tap + 2 * p), split(first_tap + 2 * p + 1), 0, total), axis=1
        )
        part = jnp.dot(cot_all, patches, preferred_element_type=F32)
        if fused:
            part = part.reshape(2, chips * per, 2 * cin)
            d32[p] = part
            d16[p] = part.astype(BF16)
            core_copy(p).start()
            if p > 0:
                core_sum(p - 1)
        else:
            gw_ref[:, p * 2 * cin : (p + 1) * 2 * cin] = part

    act_grad = jnp.zeros((rows, cin), F32)
    for tap in range(27):
        k, a, b = split(tap)
        block = cext[2 - b, 2 - k : 2 - k + frames, 2 - a : 2 - a + height, :, :].reshape(rows, cout)
        if k < 2:
            scale = mask[k, pl.ds(z * frames + 2 - k, frames)].reshape(rows, 128)
            block = jnp.concatenate(
                [block[:, m * 128 : (m + 1) * 128] * scale for m in range(chunks)], axis=1
            )
        act_grad = act_grad + lax.dot_general(
            block, w_ref[tap * cin : (tap + 1) * cin, :], (((1,), (1,)), ((), ())),
            preferred_element_type=F32,
        )
        if fused and tap == 2:
            core_sum(pairs - 1)
    d_normed = act_grad * (sig * (1.0 + normed * (1.0 - sig))) * gain
    along = jnp.sum(d_normed * video, axis=1, keepdims=True) / cin
    vgrad_ref[...] = (inv * d_normed - video * (inv * inv * inv * along)).astype(BF16)

    if fused:
        scale = 1.0 / math.sqrt(dp * total * pixels)
        sums = []
        for p in range(pairs):
            own = s32[p, chip]
            for r in range(1, chips):
                chip_copy(p, r).wait_recv()
                own = own + r2[p, r - 1].astype(F32)
            sums.append(own * scale)
        wide = jnp.concatenate(sums, axis=1)
        skip = z * slab - first_tap * cin
        wide = pltpu.roll(wide, pairs * 2 * cin - skip, axis=1)
        gw_ref[...] = wide[:, :slab]
        for p in range(pairs):
            core_copy(p).wait_send()
            for r in range(1, chips):
                chip_copy(p, r).wait_send()

    for step in range(tm - 1):
        @pl.when((z < tm - 1) & (z - step >= 0))
        def _():
            to_right(step, z - step).wait_send()

        @pl.when((z > 0) & (z + step <= tm - 1))
        def _():
            to_left(step, z + step).wait_send()


def shards(sizes, clip_video, clip_ids, norm_gain, conv_weight, out_cotangent):
    tm, dp = sizes
    unused, frames, height, width, cin = clip_video.shape
    krows, cout = conv_weight.shape
    rows = frames * height * width
    total = tm * frames
    slab = krows // tm
    per = cout // dp
    spans = [-(-(z * slab % cin + slab) // cin) for z in range(tm)]
    pairs = (max(spans) + 1) // 2
    fused = per % 16 == 0
    chips = dp // 2
    chunks = cout // 128
    wide = 2 * pairs * cin
    gw_shape = (per, slab) if fused else (cout, wide)
    cfg = (tm, dp, frames, height, width, cin, cout, slab, pairs, fused)
    side = (pairs, 2, cout // 2, 2 * cin) if fused else (1, 2, 8, 128)
    ends = (pairs, chips, per, 2 * cin) if fused else (1, 1, 16, 128)
    vmem = pl.BlockSpec(memory_space=pltpu.VMEM)
    conv, vgrad, gw = pl.pallas_call(
        functools.partial(kernel, cfg),
        out_shape=(
            jax.ShapeDtypeStruct((rows, cout), BF16),
            jax.ShapeDtypeStruct((rows, cin), BF16),
            jax.ShapeDtypeStruct(gw_shape, F32),
        ),
        in_specs=[vmem, pl.BlockSpec(memory_space=pltpu.SMEM), vmem, pl.BlockSpec(memory_space=pl.ANY), vmem],
        out_specs=(vmem, vmem, vmem),
        scratch_shapes=[
            pltpu.VMEM((krows, cout), BF16),
            pltpu.VMEM((tm, (chunks + 1) * rows + rows // 2, 128), BF16),
            pltpu.VMEM((2, 3, total + 3, height + 2, width, 256), BF16),
            pltpu.VMEM((3, 2 * frames, height + 2, width, cout), BF16),
            pltpu.VMEM((4, total + 2, height * width, 128), BF16),
            pltpu.VMEM((tm, cout, rows), BF16),
            pltpu.VMEM(side, F32),
            pltpu.VMEM(side, BF16),
            pltpu.VMEM(side[:1] + side[2:], BF16),
            pltpu.VMEM(ends, BF16),
            pltpu.VMEM(ends, F32),
            pltpu.VMEM(ends, BF16),
            pltpu.SemaphoreType.DMA,
            pltpu.SemaphoreType.DMA((tm,)),
            pltpu.SemaphoreType.DMA((tm,)),
            pltpu.SemaphoreType.DMA((tm,)),
            pltpu.SemaphoreType.DMA((tm,)),
            pltpu.SemaphoreType.DMA((pairs,)),
            pltpu.SemaphoreType.DMA((pairs,)),
            pltpu.SemaphoreType.DMA((pairs, chips)),
            pltpu.SemaphoreType.DMA((pairs, chips)),
        ],
        compiler_params=pltpu.CompilerParams(
            collective_id=0, has_side_effects=True, vmem_limit_bytes=56 * 1024 * 1024
        ),
    )(
        clip_video.reshape(rows, cin),
        clip_ids,
        norm_gain.reshape(1, cin),
        conv_weight,
        out_cotangent.reshape(rows, cout),
    )
    if fused:
        grad_weight = gw.T
    else:
        scale = 1.0 / math.sqrt(dp * total * height * width)
        mine = lax.psum_scatter(gw * scale, "dp", scatter_dimension=0, tiled=True)
        z = lax.axis_index("tm")
        grad_weight = lax.dynamic_slice_in_dim(mine, z * slab % cin, slab, 1).T
    return (
        conv.reshape(1, frames, height, width, cout),
        vgrad.reshape(1, frames, height, width, cin),
        grad_weight,
    )


def solution(mesh):
    in_specs = (
        P("dp", "tm", None, None, None),
        P("dp", None),
        P(),
        P(),
        P("dp", "tm", None, None, None),
    )
    out_specs = (P("dp", "tm", None, None, None), P("dp", "tm", None, None, None), P("tm", "dp"))
    sizes = (mesh.shape["tm"], mesh.shape["dp"])
    return jax.shard_map(
        functools.partial(shards, sizes), mesh=mesh, in_specs=in_specs, out_specs=out_specs, check_vma=False
    )
```

```python
import functools
import math

import jax
import jax.numpy as jnp
from jax import lax
from jax.experimental import pallas as pl
from jax.experimental.pallas import tpu as pltpu
from jax.sharding import PartitionSpec as P

MESH = pl.DeviceIdType.MESH
F32 = jnp.float32
BF16 = jnp.bfloat16


def half_roll(x):
    return pltpu.roll(x, 64, axis=1)


def shifted(x, width, b):
    if b == 1:
        return x
    rows = x.shape[0]
    column = lax.broadcasted_iota(jnp.int32, x.shape, 0) % width
    if b == 0:
        return jnp.where(column == 0, 0.0, pltpu.roll(x, 1, axis=0))
    return jnp.where(column == width - 1, 0.0, pltpu.roll(x, rows - 1, axis=0))


def kernel(
    cfg, video_ref, ids_ref, gain_ref, w_hbm, cot_ref, conv_ref, vgrad_ref, gw_ref,
    w_ref, pay, ext, cext, mask, cot_t, d32, d16, r1, s16, s32, r2,
    w_sem, send_r, send_l, recv_r, recv_l, core_send, core_recv, chip_send, chip_recv,
):
    tm, dp, frames, height, width, cin, cout, slab, pairs, fused = cfg
    total = tm * frames
    rows = frames * height * width
    pixels = height * width
    chunks = cout // 128
    z = lax.axis_index("tm")
    j = lax.axis_index("dp")
    core = j % 2
    chip = j // 2
    chips = dp // 2
    per = cout // dp

    w_copy = pltpu.make_async_copy(w_hbm, w_ref, w_sem)
    w_copy.start()

    barrier = pltpu.get_barrier_semaphore()

    def greet(where):
        pl.semaphore_signal(barrier, inc=1, device_id=where, device_id_type=MESH)

    @pl.when(z > 0)
    def _():
        greet((z - 1, j))

    @pl.when(z < tm - 1)
    def _():
        greet((z + 1, j))

    if fused:
        greet((z, chip * 2 + 1 - core))
        for r in range(1, chips):
            greet((z, (chip + r) % chips * 2 + core))

    video = video_ref[...].astype(F32)
    gain = gain_ref[...]
    mean_square = jnp.sum(video * video, axis=1, keepdims=True) / cin
    inv = lax.rsqrt(mean_square + 1e-06)
    normed = video * inv * gain
    sig = jax.nn.sigmoid(normed)
    act = (normed * sig).astype(BF16).astype(F32)
    lane = lax.broadcasted_iota(jnp.int32, (rows, 128), 1)
    low = lane < 64
    first = act[:, :128]
    second = jnp.concatenate([act[:, 128:], jnp.zeros((rows, 64), F32)], axis=1)
    half = rows // 2
    for m in range(chunks):
        pay[z, m * rows : (m + 1) * rows, :] = cot_ref[:, m * 128 : (m + 1) * 128]
    pay[z, chunks * rows : (chunks + 1) * rows, :] = first.astype(BF16)
    pay[z, (chunks + 1) * rows :, :] = (second[:half] + half_roll(second[half:])).astype(BF16)

    peers = jnp.where(z > 0, 1, 0) + jnp.where(z < tm - 1, 1, 0)
    if fused:
        peers = peers + chips
    pl.semaphore_wait(barrier, peers)

    def to_right(step, shard):
        return pltpu.make_async_remote_copy(
            src_ref=pay.at[shard], dst_ref=pay.at[shard], send_sem=send_r.at[step],
            recv_sem=recv_r.at[step], device_id=(z + 1, j), device_id_type=MESH,
        )

    def to_left(step, shard):
        return pltpu.make_async_remote_copy(
            src_ref=pay.at[shard], dst_ref=pay.at[shard], send_sem=send_l.at[step],
            recv_sem=recv_l.at[step], device_id=(z - 1, j), device_id_type=MESH,
        )

    def start_step(step):
        @pl.when((z < tm - 1) & (z - step >= 0))
        def _():
            to_right(step, z - step).start()

        @pl.when((z > 0) & (z + step <= tm - 1))
        def _():
            to_left(step, z + step).start()

    start_step(0)

    ext[...] = jnp.zeros(ext.shape, BF16)
    cext[...] = jnp.zeros(cext.shape, BF16)
    mask[...] = jnp.zeros(mask.shape, BF16)
    for t in range(total):
        for k in range(3):
            if t - 2 + k >= 0:
                same = jnp.where(ids_ref[0, t - 2 + k] == ids_ref[0, t], 1.0, 0.0)
                mask[k, t] = jnp.full((pixels, 128), same, F32).astype(BF16)

    def blocks(x):
        return x.astype(BF16).reshape(frames, height, width, 128)

    def place(shard):
        t0 = pay[shard, chunks * rows : (chunks + 1) * rows, :].astype(F32)
        pack = pay[shard, (chunks + 1) * rows :, :].astype(F32)
        plow = low[:half]
        t1 = jnp.concatenate(
            [jnp.where(plow, pack, 0.0), half_roll(jnp.where(plow, 0.0, pack))], axis=0
        )
        tiles = (
            (t0, t1),
            (half_roll(jnp.where(low, t0, 0.0)), half_roll(jnp.where(low, t1, t0))),
        )
        at = pl.ds(shard * frames + 2, frames)
        for b in range(3):
            for v in range(2):
                for n in range(2):
                    ext[v, b, at, 1 : 1 + height, :, n * 128 : (n + 1) * 128] = blocks(
                        shifted(tiles[v][n], width, b)
                    )
        turned = jnp.concatenate(
            [
                jnp.transpose(pay[shard, m * rows : (m + 1) * rows, :])
                for m in range(chunks)
            ],
            axis=0,
        )
        if fused:
            for d in range(chips):
                for e in range(2):
                    at_row = (e * chips + d) * per
                    from_row = (d * 2 + e) * per
                    cot_t[shard, at_row : at_row + per, :] = turned[from_row : from_row + per]
        else:
            cot_t[shard] = turned

    def place_cot(shard, frame):
        for m in range(chunks):
            tile = pay[shard, m * rows : (m + 1) * rows, :].astype(F32)
            for b in range(3):
                cext[b, frame : frame + frames, 1 : 1 + height, :, m * 128 : (m + 1) * 128] = blocks(
                    shifted(tile, width, b)
                )

    place(z)
    place_cot(z, 0)

    def finish_step(step):
        @pl.when(z - 1 - step >= 0)
        def _():
            to_right(step, z - 1 - step).wait_recv()

        @pl.when(z + 1 + step <= tm - 1)
        def _():
            to_left(step, z + 1 + step).wait_recv()

        if step + 1 < tm - 1:
            start_step(step + 1)

        @pl.when(z - 1 - step >= 0)
        def _():
            place(z - 1 - step)

        @pl.when(z + 1 + step <= tm - 1)
        def _():
            place(z + 1 + step)
            if step == 0:
                place_cot(z + 1, frames)

    def pair_tiles(one, two, at, count):
        n = count * pixels

        def part(v, tap):
            k, a, b = tap
            block = ext[v, b, pl.ds(at + k, count), pl.ds(a, height), :, :]
            scale = mask[k, pl.ds(at, count)].reshape(n, 128)
            block = block.reshape(n, 256)
            return block[:, :128] * scale, block[:, 128:] * scale

        a0, a1 = part(0, one)
        if two is None:
            return [a0, a1[:, : cin - 128]]
        b0, b1 = part(1, two)
        return [a0, a1 + b0, b1]

    def conv_some(taps):
        tiles = []
        for n in range(0, len(taps), 2):
            two = taps[n + 1] if n + 1 < len(taps) else None
            tiles += pair_tiles(split(taps[n]), None if two is None else split(two), z * frames, frames)
        return jnp.dot(
            jnp.concatenate(tiles, axis=1),
            w_ref[taps[0] * cin : (taps[-1] + 1) * cin, :],
            preferred_element_type=F32,
        )

    def split(tap):
        return tap // 9, tap // 3 % 3, tap % 3

    finish_step(0)
    w_copy.wait()
    groups = [list(range(n, min(n + 4, 27))) for n in range(0, 27, 4)]
    steps_left = max(tm - 2, 1)
    conv = jnp.zeros((rows, cout), F32)
    done = 0
    for step in range(1, tm):
        upto = len(groups) * step // steps_left if step <= steps_left else len(groups)
        while done < upto:
            conv = conv + conv_some(groups[done])
            done += 1
        if step < tm - 1:
            finish_step(step)
    conv_ref[...] = conv.astype(BF16)

    first_tap = z * slab // cin
    cot_all = jnp.concatenate([cot_t[s] for s in range(tm)], axis=1)

    def core_copy(p):
        return pltpu.make_async_remote_copy(
            src_ref=d16.at[p, 1 - core], dst_ref=r1.at[p], send_sem=core_send.at[p],
            recv_sem=core_recv.at[p], device_id=(z, chip * 2 + 1 - core), device_id_type=MESH,
        )

    def chip_copy(p, r):
        there = (chip + r) % chips
        return pltpu.make_async_remote_copy(
            src_ref=s16.at[p, there], dst_ref=r2.at[p, r - 1], send_sem=chip_send.at[p, r - 1],
            recv_sem=chip_recv.at[p, r - 1], device_id=(z, there * 2 + core), device_id_type=MESH,
        )

    def core_sum(p):
        core_copy(p).wait_recv()
        both = d32[p, core] + r1[p].astype(F32)
        both = both.reshape(chips, per, 2 * cin)
        s32[p] = both
        s16[p] = both.astype(BF16)
        for r in range(1, chips):
            chip_copy(p, r).start()

    for p in range(pairs):
        patches = jnp.concatenate(
            pair_tiles(split(first_tap + 2 * p), split(first_tap + 2 * p + 1), 0, total), axis=1
        )
        part = jnp.dot(cot_all, patches, preferred_element_type=F32)
        if fused:
            part = part.reshape(2, chips * per, 2 * cin)
            d32[p] = part
            d16[p] = part.astype(BF16)
            core_copy(p).start()
            if p > 0:
                core_sum(p - 1)
        else:
            gw_ref[:, p * 2 * cin : (p + 1) * 2 * cin] = part

    act_grad = jnp.zeros((rows, cin), F32)
    for tap in range(27):
        k, a, b = split(tap)
        block = cext[2 - b, 2 - k : 2 - k + frames, 2 - a : 2 - a + height, :, :].reshape(rows, cout)
        if k < 2:
            scale = mask[k, pl.ds(z * frames + 2 - k, frames)].reshape(rows, 128)
            block = jnp.concatenate(
                [block[:, m * 128 : (m + 1) * 128] * scale for m in range(chunks)], axis=1
            )
        act_grad = act_grad + lax.dot_general(
            block, w_ref[tap * cin : (tap + 1) * cin, :], (((1,), (1,)), ((), ())),
            preferred_element_type=F32,
        )
        if fused and tap == 2:
            core_sum(pairs - 1)
    d_normed = act_grad * (sig * (1.0 + normed * (1.0 - sig))) * gain
    along = jnp.sum(d_normed * video, axis=1, keepdims=True) / cin
    vgrad_ref[...] = (inv * d_normed - video * (inv * inv * inv * along)).astype(BF16)

    if fused:
        scale = 1.0 / math.sqrt(dp * total * pixels)
        sums = []
        for p in range(pairs):
            own = s32[p, chip]
            for r in range(1, chips):
                chip_copy(p, r).wait_recv()
                own = own + r2[p, r - 1].astype(F32)
            sums.append(own * scale)
        wide = jnp.concatenate(sums, axis=1)
        skip = z * slab - first_tap * cin
        wide = pltpu.roll(wide, pairs * 2 * cin - skip, axis=1)
        gw_ref[...] = wide[:, :slab]
        for p in range(pairs):
            core_copy(p).wait_send()
            for r in range(1, chips):
                chip_copy(p, r).wait_send()

    for step in range(tm - 1):
        @pl.when((z < tm - 1) & (z - step >= 0))
        def _():
            to_right(step, z - step).wait_send()

        @pl.when((z > 0) & (z + step <= tm - 1))
        def _():
            to_left(step, z + step).wait_send()


def shards(sizes, clip_video, clip_ids, norm_gain, conv_weight, out_cotangent):
    tm, dp = sizes
    unused, frames, height, width, cin = clip_video.shape
    krows, cout = conv_weight.shape
    rows = frames * height * width
    total = tm * frames
    slab = krows // tm
    per = cout // dp
    spans = [-(-(z * slab % cin + slab) // cin) for z in range(tm)]
    pairs = (max(spans) + 1) // 2
    fused = per % 16 == 0
    chips = dp // 2
    chunks = cout // 128
    wide = 2 * pairs * cin
    gw_shape = (per, slab) if fused else (cout, wide)
    cfg = (tm, dp, frames, height, width, cin, cout, slab, pairs, fused)
    side = (pairs, 2, cout // 2, 2 * cin) if fused else (1, 2, 8, 128)
    ends = (pairs, chips, per, 2 * cin) if fused else (1, 1, 16, 128)
    vmem = pl.BlockSpec(memory_space=pltpu.VMEM)
    conv, vgrad, gw = pl.pallas_call(
        functools.partial(kernel, cfg),
        out_shape=(
            jax.ShapeDtypeStruct((rows, cout), BF16),
            jax.ShapeDtypeStruct((rows, cin), BF16),
            jax.ShapeDtypeStruct(gw_shape, F32),
        ),
        in_specs=[vmem, pl.BlockSpec(memory_space=pltpu.SMEM), vmem, pl.BlockSpec(memory_space=pl.ANY), vmem],
        out_specs=(vmem, vmem, vmem),
        scratch_shapes=[
            pltpu.VMEM((krows, cout), BF16),
            pltpu.VMEM((tm, (chunks + 1) * rows + rows // 2, 128), BF16),
            pltpu.VMEM((2, 3, total + 3, height + 2, width, 256), BF16),
            pltpu.VMEM((3, 2 * frames, height + 2, width, cout), BF16),
            pltpu.VMEM((4, total + 2, height * width, 128), BF16),
            pltpu.VMEM((tm, cout, rows), BF16),
            pltpu.VMEM(side, F32),
            pltpu.VMEM(side, BF16),
            pltpu.VMEM(side[:1] + side[2:], BF16),
            pltpu.VMEM(ends, BF16),
            pltpu.VMEM(ends, F32),
            pltpu.VMEM(ends, BF16),
            pltpu.SemaphoreType.DMA,
            pltpu.SemaphoreType.DMA((tm,)),
            pltpu.SemaphoreType.DMA((tm,)),
            pltpu.SemaphoreType.DMA((tm,)),
            pltpu.SemaphoreType.DMA((tm,)),
            pltpu.SemaphoreType.DMA((pairs,)),
            pltpu.SemaphoreType.DMA((pairs,)),
            pltpu.SemaphoreType.DMA((pairs, chips)),
            pltpu.SemaphoreType.DMA((pairs, chips)),
        ],
        compiler_params=pltpu.CompilerParams(
            collective_id=0, has_side_effects=True, vmem_limit_bytes=51 * 1024 * 1024
        ),
    )(
        clip_video.reshape(rows, cin),
        clip_ids,
        norm_gain.reshape(1, cin),
        conv_weight,
        out_cotangent.reshape(rows, cout),
    )
    if fused:
        grad_weight = gw.T
    else:
        scale = 1.0 / math.sqrt(dp * total * height * width)
        mine = lax.psum_scatter(gw * scale, "dp", scatter_dimension=0, tiled=True)
        z = lax.axis_index("tm")
        grad_weight = lax.dynamic_slice_in_dim(mine, z * slab % cin, slab, 1).T
    return (
        conv.reshape(1, frames, height, width, cout),
        vgrad.reshape(1, frames, height, width, cin),
        grad_weight,
    )


def solution(mesh):
    in_specs = (
        P("dp", "tm", None, None, None),
        P("dp", None),
        P(),
        P(),
        P("dp", "tm", None, None, None),
    )
    out_specs = (P("dp", "tm", None, None, None), P("dp", "tm", None, None, None), P("tm", "dp"))
    sizes = (mesh.shape["tm"], mesh.shape["dp"])
    return jax.shard_map(
        functools.partial(shards, sizes), mesh=mesh, in_specs=in_specs, out_specs=out_specs, check_vma=False
    )
```

```python
import functools
import math

import jax
import jax.numpy as jnp
from jax import lax
from jax.experimental import pallas as pl
from jax.experimental.pallas import tpu as pltpu
from jax.sharding import PartitionSpec as P

MESH = pl.DeviceIdType.MESH
F32 = jnp.float32
BF16 = jnp.bfloat16


def half_roll(x):
    return pltpu.roll(x, 64, axis=1)


def shifted(x, width, b):
    if b == 1:
        return x
    rows = x.shape[0]
    column = lax.broadcasted_iota(jnp.int32, x.shape, 0) % width
    if b == 0:
        return jnp.where(column == 0, 0.0, pltpu.roll(x, 1, axis=0))
    return jnp.where(column == width - 1, 0.0, pltpu.roll(x, rows - 1, axis=0))


def kernel(
    cfg, video_ref, ids_ref, gain_ref, w_hbm, cot_ref, conv_ref, vgrad_ref, gw_ref,
    w_ref, pay, ext, cext, mask, cot_t, d32, d16, r1, s16, s32, r2,
    w_sem, send_r, send_l, recv_r, recv_l, core_send, core_recv, chip_send, chip_recv,
):
    tm, dp, frames, height, width, cin, cout, slab, pairs, fused = cfg
    total = tm * frames
    rows = frames * height * width
    pixels = height * width
    chunks = cout // 128
    z = lax.axis_index("tm")
    j = lax.axis_index("dp")
    core = j % 2
    chip = j // 2
    chips = dp // 2
    per = cout // dp

    w_copy = pltpu.make_async_copy(w_hbm, w_ref, w_sem)
    w_copy.start()

    barrier = pltpu.get_barrier_semaphore()

    def greet(where):
        pl.semaphore_signal(barrier, inc=1, device_id=where, device_id_type=MESH)

    @pl.when(z > 0)
    def _():
        greet((z - 1, j))

    @pl.when(z < tm - 1)
    def _():
        greet((z + 1, j))

    if fused:
        greet((z, chip * 2 + 1 - core))
        for r in range(1, chips):
            greet((z, (chip + r) % chips * 2 + core))

    video = video_ref[...].astype(F32)
    gain = gain_ref[...]
    mean_square = jnp.sum(video * video, axis=1, keepdims=True) / cin
    inv = lax.rsqrt(mean_square + 1e-06)
    normed = video * inv * gain
    sig = jax.nn.sigmoid(normed)
    act = (normed * sig).astype(BF16).astype(F32)
    lane = lax.broadcasted_iota(jnp.int32, (rows, 128), 1)
    low = lane < 64
    first = act[:, :128]
    second = jnp.concatenate([act[:, 128:], jnp.zeros((rows, 64), F32)], axis=1)
    half = rows // 2
    turned = jnp.concatenate(
        [jnp.transpose(cot_ref[:, m * 128 : (m + 1) * 128]) for m in range(chunks)], axis=0
    )
    order = [(d * 2 + e) * per for e in range(2) for d in range(chips)] if fused else [0]
    span = per if fused else cout
    for at_row, from_row in enumerate(order):
        pay[z, at_row * span : (at_row + 1) * span, :] = turned[from_row : from_row + span]
    pay[z, cout : cout + rows, :] = first.astype(BF16)
    pay[z, cout + rows :, :] = (second[:half] + half_roll(second[half:])).astype(BF16)

    peers = jnp.where(z > 0, 1, 0) + jnp.where(z < tm - 1, 1, 0)
    if fused:
        peers = peers + chips
    pl.semaphore_wait(barrier, peers)

    size = pay.shape[1] // 2

    def part_of(shard, h):
        return pay.at[shard, pl.ds(h * size, size)]

    def to_right(step, shard, h):
        return pltpu.make_async_remote_copy(
            src_ref=part_of(shard, h), dst_ref=part_of(shard, h), send_sem=send_r.at[step, h],
            recv_sem=recv_r.at[step, h], device_id=(z + 1, j), device_id_type=MESH,
        )

    def to_left(step, shard, h):
        return pltpu.make_async_remote_copy(
            src_ref=part_of(shard, h), dst_ref=part_of(shard, h), send_sem=send_l.at[step, h],
            recv_sem=recv_l.at[step, h], device_id=(z - 1, j), device_id_type=MESH,
        )

    def start_step(step, h):
        @pl.when((z < tm - 1) & (z - step >= 0))
        def _():
            to_right(step, z - step, h).start()

        @pl.when((z > 0) & (z + step <= tm - 1))
        def _():
            to_left(step, z + step, h).start()

    start_step(0, 0)
    start_step(0, 1)

    ext[...] = jnp.zeros(ext.shape, BF16)
    cext[...] = jnp.zeros(cext.shape, BF16)
    cot_t[...] = jnp.zeros(cot_t.shape, BF16)
    mask[...] = jnp.zeros(mask.shape, BF16)
    for t in range(total):
        for k in range(3):
            if t - 2 + k >= 0:
                same = jnp.where(ids_ref[0, t - 2 + k] == ids_ref[0, t], 1.0, 0.0)
                mask[k, t] = jnp.full((pixels, 128), same, F32).astype(BF16)

    def blocks(x):
        return x.astype(BF16).reshape(frames, height, width, 128)

    def place(shard):
        t0 = pay[shard, cout : cout + rows, :].astype(F32)
        pack = pay[shard, cout + rows :, :].astype(F32)
        plow = low[:half]
        t1 = jnp.concatenate(
            [jnp.where(plow, pack, 0.0), half_roll(jnp.where(plow, 0.0, pack))], axis=0
        )
        tiles = (
            (t0, t1),
            (half_roll(jnp.where(low, t0, 0.0)), half_roll(jnp.where(low, t1, t0))),
        )
        at = pl.ds(shard * frames + 2, frames)
        for b in range(3):
            for v in range(2):
                for n in range(2):
                    ext[v, b, at, 1 : 1 + height, :, n * 128 : (n + 1) * 128] = blocks(
                        shifted(tiles[v][n], width, b)
                    )
        cot_t[shard] = pay[shard, :cout, :]

    def place_cot(tiles, frame):
        for m in range(chunks):
            tile = tiles[m].astype(F32)
            for b in range(3):
                cext[b, frame : frame + frames, 1 : 1 + height, :, m * 128 : (m + 1) * 128] = blocks(
                    shifted(tile, width, b)
                )

    def next_tiles():
        rows_of = {at: pay[z + 1, n * span : (n + 1) * span, :] for n, at in enumerate(order)}
        natural = jnp.concatenate([rows_of[at] for at in sorted(rows_of)], axis=0)
        return [jnp.transpose(natural[m * 128 : (m + 1) * 128]) for m in range(chunks)]

    place(z)
    place_cot([cot_ref[:, m * 128 : (m + 1) * 128] for m in range(chunks)], 0)

    def finish_step(step):
        for h in range(2):
            @pl.when(z - 1 - step >= 0)
            def _():
                to_right(step, z - 1 - step, h).wait_recv()

            @pl.when(z + 1 + step <= tm - 1)
            def _():
                to_left(step, z + 1 + step, h).wait_recv()

            if step + 1 < tm - 1:
                start_step(step + 1, h)

        @pl.when(z - 1 - step >= 0)
        def _():
            place(z - 1 - step)

        @pl.when(z + 1 + step <= tm - 1)
        def _():
            place(z + 1 + step)
            if step == 0:
                place_cot(next_tiles(), frames)

    def pair_tiles(one, two, at, count):
        n = count * pixels

        def part(v, tap):
            k, a, b = tap
            block = ext[v, b, pl.ds(at + k, count), pl.ds(a, height), :, :]
            scale = mask[k, pl.ds(at, count)].reshape(n, 128)
            block = block.reshape(n, 256)
            return block[:, :128] * scale, block[:, 128:] * scale

        a0, a1 = part(0, one)
        if two is None:
            return [a0, a1[:, : cin - 128]]
        b0, b1 = part(1, two)
        return [a0, a1 + b0, b1]

    def conv_some(taps):
        tiles = []
        for n in range(0, len(taps), 2):
            two = taps[n + 1] if n + 1 < len(taps) else None
            tiles += pair_tiles(split(taps[n]), None if two is None else split(two), z * frames, frames)
        return jnp.dot(
            jnp.concatenate(tiles, axis=1),
            w_ref[taps[0] * cin : (taps[-1] + 1) * cin, :],
            preferred_element_type=F32,
        )

    def split(tap):
        return tap // 9, tap // 3 % 3, tap % 3

    def conv_range(start, stop):
        found = jnp.zeros((rows, cout), F32)
        for n in range(start, stop, 4):
            found = found + conv_some(list(range(n, min(n + 4, stop))))
        return found

    def grad_range(start, stop):
        found = jnp.zeros((rows, cin), F32)
        for tap in range(start, stop):
            k, a, b = split(tap)
            block = cext[2 - b, 2 - k : 2 - k + frames, 2 - a : 2 - a + height, :, :].reshape(rows, cout)
            if k < 2:
                scale = mask[k, pl.ds(z * frames + 2 - k, frames)].reshape(rows, 128)
                block = jnp.concatenate(
                    [block[:, m * 128 : (m + 1) * 128] * scale for m in range(chunks)], axis=1
                )
            found = found + lax.dot_general(
                block, w_ref[tap * cin : (tap + 1) * cin, :], (((1,), (1,)), ((), ())),
                preferred_element_type=F32,
            )
        return found

    w_copy.wait()
    conv = conv_range(18, 27)
    act_grad = grad_range(18, 27)
    finish_step(0)
    conv = conv + conv_range(0, 18)
    conv_ref[...] = conv.astype(BF16)
    for step in range(1, tm - 2):
        finish_step(step)

    first_tap = z * slab // cin

    def core_copy(p):
        return pltpu.make_async_remote_copy(
            src_ref=d16.at[p], dst_ref=r1.at[p], send_sem=core_send.at[p],
            recv_sem=core_recv.at[p], device_id=(z, chip * 2 + 1 - core), device_id_type=MESH,
        )

    def chip_copy(p, r):
        there = (chip + r) % chips
        return pltpu.make_async_remote_copy(
            src_ref=s16.at[p, there], dst_ref=r2.at[p, r - 1], send_sem=chip_send.at[p, r - 1],
            recv_sem=chip_recv.at[p, r - 1], device_id=(z, there * 2 + core), device_id_type=MESH,
        )

    def core_sum(p):
        core_copy(p).wait_recv()
        both = d32[p, core] + r1[p].astype(F32)
        both = both.reshape(chips, per, 2 * cin)
        s32[p] = both
        s16[p] = both.astype(BF16)
        for r in range(1, chips):
            chip_copy(p, r).start()

    def weight_part(p, cot_rows, at, count):
        one = first_tap + 2 * p
        patches = jnp.concatenate(pair_tiles(split(one), split(one + 1), at, count), axis=1)
        return jnp.dot(cot_rows, patches, preferred_element_type=F32).reshape(d32.shape[1:])

    cot_all = jnp.concatenate([cot_t[s] for s in range(tm)], axis=1)
    for p in range(pairs):
        d32[p] = weight_part(p, cot_all, 0, total)
    finish_step(tm - 2)
    last = tm - 1 - z
    for p in range(pairs):
        @pl.when((z == 0) | (z == tm - 1))
        def _():
            d32[p] = d32[p] + weight_part(p, cot_t[last], last * frames, frames)

        if fused:
            d16[p] = d32[p, 1 - core].astype(BF16)
            core_copy(p).start()
            if p > 0:
                core_sum(p - 1)
        else:
            gw_ref[:, p * 2 * cin : (p + 1) * 2 * cin] = d32[p].reshape(cout, 2 * cin)
    act_grad = act_grad + grad_range(0, 3)
    if fused:
        core_sum(pairs - 1)
    act_grad = act_grad + grad_range(3, 18)
    d_normed = act_grad * (sig * (1.0 + normed * (1.0 - sig))) * gain
    along = jnp.sum(d_normed * video, axis=1, keepdims=True) / cin
    vgrad_ref[...] = (inv * d_normed - video * (inv * inv * inv * along)).astype(BF16)

    if fused:
        scale = 1.0 / math.sqrt(dp * total * pixels)
        sums = []
        for p in range(pairs):
            own = s32[p, chip]
            for r in range(1, chips):
                chip_copy(p, r).wait_recv()
                own = own + r2[p, r - 1].astype(F32)
            sums.append(own * scale)
        wide = jnp.concatenate(sums, axis=1)
        skip = z * slab - first_tap * cin
        wide = pltpu.roll(wide, pairs * 2 * cin - skip, axis=1)
        gw_ref[...] = wide[:, :slab]
        for p in range(pairs):
            core_copy(p).wait_send()
            for r in range(1, chips):
                chip_copy(p, r).wait_send()

    for step in range(tm - 1):
        @pl.when((z < tm - 1) & (z - step >= 0))
        def _():
            for h in range(2):
                to_right(step, z - step, h).wait_send()

        @pl.when((z > 0) & (z + step <= tm - 1))
        def _():
            for h in range(2):
                to_left(step, z + step, h).wait_send()


def shards(sizes, clip_video, clip_ids, norm_gain, conv_weight, out_cotangent):
    tm, dp = sizes
    unused, frames, height, width, cin = clip_video.shape
    krows, cout = conv_weight.shape
    rows = frames * height * width
    total = tm * frames
    slab = krows // tm
    per = cout // dp
    spans = [-(-(z * slab % cin + slab) // cin) for z in range(tm)]
    pairs = (max(spans) + 1) // 2
    fused = per % 16 == 0
    chips = dp // 2
    chunks = cout // 128
    wide = 2 * pairs * cin
    gw_shape = (per, slab) if fused else (cout, wide)
    cfg = (tm, dp, frames, height, width, cin, cout, slab, pairs, fused)
    side = (pairs, 2, cout // 2, 2 * cin)
    one_side = (pairs, cout // 2, 2 * cin) if fused else (1, 16, 128)
    ends = (pairs, chips, per, 2 * cin) if fused else (1, 1, 16, 128)
    vmem = pl.BlockSpec(memory_space=pltpu.VMEM)
    hbm = pltpu.HBM
    pinned = [
        pltpu.with_memory_space_constraint(x, hbm)
        for x in (
            clip_video.reshape(rows, cin),
            norm_gain.reshape(1, cin),
            conv_weight,
            out_cotangent.reshape(rows, cout),
            clip_ids,
        )
    ]
    conv, vgrad, gw = pl.pallas_call(
        functools.partial(kernel, cfg),
        out_shape=(
            jax.ShapeDtypeStruct((rows, cout), BF16),
            jax.ShapeDtypeStruct((rows, cin), BF16),
            jax.ShapeDtypeStruct(gw_shape, F32),
        ),
        in_specs=[vmem, pl.BlockSpec(memory_space=pltpu.SMEM), vmem, pl.BlockSpec(memory_space=pl.ANY), vmem],
        out_specs=(vmem, vmem, vmem),
        scratch_shapes=[
            pltpu.VMEM((krows, cout), BF16),
            pltpu.VMEM((tm, (chunks + 1) * rows + rows // 2, 128), BF16),
            pltpu.VMEM((2, 3, total + 3, height + 2, width, 256), BF16),
            pltpu.VMEM((3, 2 * frames, height + 2, width, cout), BF16),
            pltpu.VMEM((4, total + 2, height * width, 128), BF16),
            pltpu.VMEM((tm, cout, rows), BF16),
            pltpu.VMEM(side, F32),
            pltpu.VMEM(one_side, BF16),
            pltpu.VMEM(one_side, BF16),
            pltpu.VMEM(ends, BF16),
            pltpu.VMEM(ends, F32),
            pltpu.VMEM(ends, BF16),
            pltpu.SemaphoreType.DMA,
            pltpu.SemaphoreType.DMA((tm, 2)),
            pltpu.SemaphoreType.DMA((tm, 2)),
            pltpu.SemaphoreType.DMA((tm, 2)),
            pltpu.SemaphoreType.DMA((tm, 2)),
            pltpu.SemaphoreType.DMA((pairs,)),
            pltpu.SemaphoreType.DMA((pairs,)),
            pltpu.SemaphoreType.DMA((pairs, chips)),
            pltpu.SemaphoreType.DMA((pairs, chips)),
        ],
        compiler_params=pltpu.CompilerParams(
            collective_id=0, has_side_effects=True, vmem_limit_bytes=40 * 1024 * 1024
        ),
    )(
        pinned[0],
        pinned[4],
        *pinned[1:4],
    )
    if fused:
        grad_weight = gw.T
    else:
        scale = 1.0 / math.sqrt(dp * total * height * width)
        mine = lax.psum_scatter(gw * scale, "dp", scatter_dimension=0, tiled=True)
        z = lax.axis_index("tm")
        grad_weight = lax.dynamic_slice_in_dim(mine, z * slab % cin, slab, 1).T
    return (
        conv.reshape(1, frames, height, width, cout),
        vgrad.reshape(1, frames, height, width, cin),
        grad_weight,
    )


def solution(mesh):
    in_specs = (
        P("dp", "tm", None, None, None),
        P("dp", None),
        P(),
        P(),
        P("dp", "tm", None, None, None),
    )
    out_specs = (P("dp", "tm", None, None, None), P("dp", "tm", None, None, None), P("tm", "dp"))
    sizes = (mesh.shape["tm"], mesh.shape["dp"])
    return jax.shard_map(
        functools.partial(shards, sizes), mesh=mesh, in_specs=in_specs, out_specs=out_specs, check_vma=False
    )
```

```python
import functools
import math

import jax
import jax.numpy as jnp
from jax import lax
from jax.experimental import pallas as pl
from jax.experimental.pallas import tpu as pltpu
from jax.sharding import PartitionSpec as P

MESH = pl.DeviceIdType.MESH
F32 = jnp.float32
BF16 = jnp.bfloat16


def half_roll(x):
    return pltpu.roll(x, 64, axis=1)


def shifted(x, width, b):
    if b == 1:
        return x
    rows = x.shape[0]
    column = lax.broadcasted_iota(jnp.int32, x.shape, 0) % width
    if b == 0:
        return jnp.where(column == 0, 0.0, pltpu.roll(x, 1, axis=0))
    return jnp.where(column == width - 1, 0.0, pltpu.roll(x, rows - 1, axis=0))


def kernel(
    cfg, video_ref, ids_ref, gain_ref, w_hbm, cot_ref, conv_ref, vgrad_ref, gw_ref,
    w_ref, pay, ext, cext, mask, cot_t, d32, d16, r1, s16, s32, r2,
    w_sem, send_r, send_l, recv_r, recv_l, core_send, core_recv, chip_send, chip_recv,
):
    tm, dp, frames, height, width, cin, cout, slab, pairs, fused = cfg
    total = tm * frames
    rows = frames * height * width
    pixels = height * width
    chunks = cout // 128
    z = lax.axis_index("tm")
    j = lax.axis_index("dp")
    core = j % 2
    chip = j // 2
    chips = dp // 2
    per = cout // dp

    w_copy = pltpu.make_async_copy(w_hbm, w_ref, w_sem)
    w_copy.start()

    barrier = pltpu.get_barrier_semaphore()

    def greet(where):
        pl.semaphore_signal(barrier, inc=1, device_id=where, device_id_type=MESH)

    @pl.when(z > 0)
    def _():
        greet((z - 1, j))

    @pl.when(z < tm - 1)
    def _():
        greet((z + 1, j))

    if fused:
        greet((z, chip * 2 + 1 - core))
        for r in range(1, chips):
            greet((z, (chip + r) % chips * 2 + core))

    video = video_ref[...].astype(F32)
    gain = gain_ref[...]
    mean_square = jnp.sum(video * video, axis=1, keepdims=True) / cin
    inv = lax.rsqrt(mean_square + 1e-06)
    normed = video * inv * gain
    sig = jax.nn.sigmoid(normed)
    act = (normed * sig).astype(BF16).astype(F32)
    lane = lax.broadcasted_iota(jnp.int32, (rows, 128), 1)
    low = lane < 64
    first = act[:, :128]
    second = jnp.concatenate([act[:, 128:], jnp.zeros((rows, 64), F32)], axis=1)
    half = rows // 2
    turned = jnp.concatenate(
        [jnp.transpose(cot_ref[:, m * 128 : (m + 1) * 128]) for m in range(chunks)], axis=0
    )
    order = [(d * 2 + e) * per for e in range(2) for d in range(chips)] if fused else [0]
    span = per if fused else cout
    for at_row, from_row in enumerate(order):
        pay[z, at_row * span : (at_row + 1) * span, :] = turned[from_row : from_row + span]
    pay[z, cout : cout + rows, :] = first.astype(BF16)
    pay[z, cout + rows :, :] = (second[:half] + half_roll(second[half:])).astype(BF16)

    peers = jnp.where(z > 0, 1, 0) + jnp.where(z < tm - 1, 1, 0)
    if fused:
        peers = peers + chips
    pl.semaphore_wait(barrier, peers)

    size = pay.shape[1] // 2

    def part_of(shard, h):
        return pay.at[shard, pl.ds(h * size, size)]

    def to_right(step, shard, h):
        return pltpu.make_async_remote_copy(
            src_ref=part_of(shard, h), dst_ref=part_of(shard, h), send_sem=send_r.at[step, h],
            recv_sem=recv_r.at[step, h], device_id=(z + 1, j), device_id_type=MESH,
        )

    def to_left(step, shard, h):
        return pltpu.make_async_remote_copy(
            src_ref=part_of(shard, h), dst_ref=part_of(shard, h), send_sem=send_l.at[step, h],
            recv_sem=recv_l.at[step, h], device_id=(z - 1, j), device_id_type=MESH,
        )

    def start_step(step, h):
        @pl.when((z < tm - 1) & (z - step >= 0))
        def _():
            to_right(step, z - step, h).start()

        @pl.when((z > 0) & (z + step <= tm - 1))
        def _():
            to_left(step, z + step, h).start()

    start_step(0, 0)
    start_step(0, 1)

    ext[...] = jnp.zeros(ext.shape, BF16)
    cext[...] = jnp.zeros(cext.shape, BF16)
    cot_t[...] = jnp.zeros(cot_t.shape, BF16)
    mask[...] = jnp.zeros(mask.shape, BF16)
    for t in range(total):
        for k in range(3):
            if t - 2 + k >= 0:
                same = jnp.where(ids_ref[0, t - 2 + k] == ids_ref[0, t], 1.0, 0.0)
                mask[k, t] = jnp.full((pixels, 128), same, F32).astype(BF16)

    def blocks(x):
        return x.astype(BF16).reshape(frames, height, width, 128)

    def place(shard):
        t0 = pay[shard, cout : cout + rows, :].astype(F32)
        pack = pay[shard, cout + rows :, :].astype(F32)
        plow = low[:half]
        t1 = jnp.concatenate(
            [jnp.where(plow, pack, 0.0), half_roll(jnp.where(plow, 0.0, pack))], axis=0
        )
        tiles = (
            (t0, t1),
            (half_roll(jnp.where(low, t0, 0.0)), half_roll(jnp.where(low, t1, t0))),
        )
        at = pl.ds(shard * frames + 2, frames)
        for b in range(3):
            for v in range(2):
                for n in range(2):
                    ext[v, b, at, 1 : 1 + height, :, n * 128 : (n + 1) * 128] = blocks(
                        shifted(tiles[v][n], width, b)
                    )
        cot_t[shard] = pay[shard, :cout, :]

    def place_cot(tiles, frame):
        for m in range(chunks):
            tile = tiles[m].astype(F32)
            for b in range(3):
                cext[b, frame : frame + frames, 1 : 1 + height, :, m * 128 : (m + 1) * 128] = blocks(
                    shifted(tile, width, b)
                )

    def next_tiles():
        rows_of = {at: pay[z + 1, n * span : (n + 1) * span, :] for n, at in enumerate(order)}
        natural = jnp.concatenate([rows_of[at] for at in sorted(rows_of)], axis=0)
        return [jnp.transpose(natural[m * 128 : (m + 1) * 128]) for m in range(chunks)]

    place(z)
    place_cot([cot_ref[:, m * 128 : (m + 1) * 128] for m in range(chunks)], 0)

    def pass_on(step, h):
        @pl.when(z - 1 - step >= 0)
        def _():
            to_right(step, z - 1 - step, h).wait_recv()

        @pl.when(z + 1 + step <= tm - 1)
        def _():
            to_left(step, z + 1 + step, h).wait_recv()

        if step + 1 < tm - 1:
            start_step(step + 1, h)

    def lay_out(step):
        @pl.when(z - 1 - step >= 0)
        def _():
            place(z - 1 - step)

        @pl.when(z + 1 + step <= tm - 1)
        def _():
            place(z + 1 + step)
            if step == 0:
                place_cot(next_tiles(), frames)

    def pair_tiles(one, two, at, count):
        n = count * pixels

        def part(v, tap):
            k, a, b = tap
            block = ext[v, b, pl.ds(at + k, count), pl.ds(a, height), :, :]
            scale = mask[k, pl.ds(at, count)].reshape(n, 128)
            block = block.reshape(n, 256)
            return block[:, :128] * scale, block[:, 128:] * scale

        a0, a1 = part(0, one)
        if two is None:
            return [a0, a1[:, : cin - 128]]
        b0, b1 = part(1, two)
        return [a0, a1 + b0, b1]

    def conv_some(taps):
        tiles = []
        for n in range(0, len(taps), 2):
            two = taps[n + 1] if n + 1 < len(taps) else None
            tiles += pair_tiles(split(taps[n]), None if two is None else split(two), z * frames, frames)
        return jnp.dot(
            jnp.concatenate(tiles, axis=1),
            w_ref[taps[0] * cin : (taps[-1] + 1) * cin, :],
            preferred_element_type=F32,
        )

    def split(tap):
        return tap // 9, tap // 3 % 3, tap % 3

    def conv_range(start, stop):
        found = jnp.zeros((rows, cout), F32)
        for n in range(start, stop, 4):
            found = found + conv_some(list(range(n, min(n + 4, stop))))
        return found

    def grad_range(start, stop):
        found = jnp.zeros((rows, cin), F32)

        def columns(tap):
            k, a, b = split(tap)
            block = cext[2 - b, 2 - k : 2 - k + frames, 2 - a : 2 - a + height, :, :].reshape(rows, cout)
            if k == 2:
                return [block]
            scale = mask[k, pl.ds(z * frames + 2 - k, frames)].reshape(rows, 128)
            return [block[:, m * 128 : (m + 1) * 128] * scale for m in range(chunks)]

        for first in range(start, stop, 2):
            taps = range(first, min(first + 2, stop))
            found = found + lax.dot_general(
                jnp.concatenate([tile for tap in taps for tile in columns(tap)], axis=1),
                jnp.concatenate([w_ref[tap * cin : (tap + 1) * cin, :] for tap in taps], axis=1),
                (((1,), (1,)), ((), ())),
                preferred_element_type=F32,
            )
        return found

    w_copy.wait()
    conv = conv_range(18, 27)
    pass_on(0, 0)
    act_grad = grad_range(18, 24)
    pass_on(0, 1)
    lay_out(0)
    conv = conv + conv_range(0, 8)
    if tm > 3:
        pass_on(1, 0)
    conv = conv + conv_range(8, 16)
    for step in range(1, tm - 2):
        if step > 1:
            pass_on(step, 0)
        pass_on(step, 1)
        lay_out(step)
    conv_ref[...] = (conv + conv_range(16, 18)).astype(BF16)

    first_tap = z * slab // cin

    def core_copy(p):
        return pltpu.make_async_remote_copy(
            src_ref=d16.at[p], dst_ref=r1.at[p], send_sem=core_send.at[p],
            recv_sem=core_recv.at[p], device_id=(z, chip * 2 + 1 - core), device_id_type=MESH,
        )

    def chip_copy(p, r):
        there = (chip + r) % chips
        return pltpu.make_async_remote_copy(
            src_ref=s16.at[p, there], dst_ref=r2.at[p, r - 1], send_sem=chip_send.at[p, r - 1],
            recv_sem=chip_recv.at[p, r - 1], device_id=(z, there * 2 + core), device_id_type=MESH,
        )

    def core_sum(p):
        core_copy(p).wait_recv()
        both = d32[p, core] + r1[p].astype(F32)
        both = both.reshape(chips, per, 2 * cin)
        s32[p] = both
        s16[p] = both.astype(BF16)
        for r in range(1, chips):
            chip_copy(p, r).start()

    def weight_part(p, cot_rows, at, count):
        one = first_tap + 2 * p
        patches = jnp.concatenate(pair_tiles(split(one), split(one + 1), at, count), axis=1)
        return jnp.dot(cot_rows, patches, preferred_element_type=F32).reshape(d32.shape[1:])

    early = max(pairs - 1, 1)
    cot_all = jnp.concatenate([cot_t[s] for s in range(tm)], axis=1)
    for p in range(early):
        d32[p] = weight_part(p, cot_all, 0, total)
    pass_on(tm - 2, 0)
    pass_on(tm - 2, 1)
    lay_out(tm - 2)
    last = tm - 1 - z
    for p in range(pairs):
        if p < early:
            @pl.when((z == 0) | (z == tm - 1))
            def _():
                d32[p] = d32[p] + weight_part(p, cot_t[last], last * frames, frames)
        else:
            cot_all = jnp.concatenate([cot_t[s] for s in range(tm)], axis=1)
            d32[p] = weight_part(p, cot_all, 0, total)

        if fused:
            d16[p] = d32[p, 1 - core].astype(BF16)
            core_copy(p).start()
            if p > 0:
                core_sum(p - 1)
        else:
            gw_ref[:, p * 2 * cin : (p + 1) * 2 * cin] = d32[p].reshape(cout, 2 * cin)
    act_grad = act_grad + grad_range(24, 27)
    if fused:
        core_sum(pairs - 1)
    act_grad = act_grad + grad_range(0, 18)
    d_normed = act_grad * (sig * (1.0 + normed * (1.0 - sig))) * gain
    along = jnp.sum(d_normed * video, axis=1, keepdims=True) / cin
    vgrad_ref[...] = (inv * d_normed - video * (inv * inv * inv * along)).astype(BF16)

    if fused:
        scale = 1.0 / math.sqrt(dp * total * pixels)
        sums = []
        for p in range(pairs):
            own = s32[p, chip]
            for r in range(1, chips):
                chip_copy(p, r).wait_recv()
                own = own + r2[p, r - 1].astype(F32)
            sums.append(own * scale)
        wide = jnp.concatenate(sums, axis=1)
        skip = z * slab - first_tap * cin
        wide = pltpu.roll(wide, pairs * 2 * cin - skip, axis=1)
        gw_ref[...] = wide[:, :slab]
        for p in range(pairs):
            core_copy(p).wait_send()
            for r in range(1, chips):
                chip_copy(p, r).wait_send()

    for step in range(tm - 1):
        @pl.when((z < tm - 1) & (z - step >= 0))
        def _():
            for h in range(2):
                to_right(step, z - step, h).wait_send()

        @pl.when((z > 0) & (z + step <= tm - 1))
        def _():
            for h in range(2):
                to_left(step, z + step, h).wait_send()


def emit(*refs):
    count = len(refs) // 2
    sems = refs[-1]
    copies = [pltpu.make_async_copy(refs[n], refs[count + n], sems.at[n]) for n in range(count)]
    for copy in copies:
        copy.start()
    for copy in copies:
        copy.wait()


def shards(sizes, clip_video, clip_ids, norm_gain, conv_weight, out_cotangent):
    tm, dp = sizes
    unused, frames, height, width, cin = clip_video.shape
    krows, cout = conv_weight.shape
    rows = frames * height * width
    total = tm * frames
    slab = krows // tm
    per = cout // dp
    spans = [-(-(z * slab % cin + slab) // cin) for z in range(tm)]
    pairs = (max(spans) + 1) // 2
    fused = per % 16 == 0
    chips = dp // 2
    chunks = cout // 128
    wide = 2 * pairs * cin
    gw_shape = (per, slab) if fused else (cout, wide)
    cfg = (tm, dp, frames, height, width, cin, cout, slab, pairs, fused)
    side = (pairs, 2, cout // 2, 2 * cin)
    one_side = (pairs, cout // 2, 2 * cin) if fused else (1, 16, 128)
    ends = (pairs, chips, per, 2 * cin) if fused else (1, 1, 16, 128)
    vmem = pl.BlockSpec(memory_space=pltpu.VMEM)
    hbm = pltpu.HBM
    pinned = [
        pltpu.with_memory_space_constraint(x, hbm)
        for x in (
            clip_video.reshape(rows, cin),
            norm_gain.reshape(1, cin),
            conv_weight,
            out_cotangent.reshape(rows, cout),
            clip_ids,
        )
    ]
    conv, vgrad, gw = pl.pallas_call(
        functools.partial(kernel, cfg),
        out_shape=(
            jax.ShapeDtypeStruct((rows, cout), BF16),
            jax.ShapeDtypeStruct((rows, cin), BF16),
            jax.ShapeDtypeStruct(gw_shape, F32),
        ),
        in_specs=[vmem, pl.BlockSpec(memory_space=pltpu.SMEM), vmem, pl.BlockSpec(memory_space=pl.ANY), vmem],
        out_specs=(vmem, vmem, vmem),
        scratch_shapes=[
            pltpu.VMEM((krows, cout), BF16),
            pltpu.VMEM((tm, (chunks + 1) * rows + rows // 2, 128), BF16),
            pltpu.VMEM((2, 3, total + 3, height + 2, width, 256), BF16),
            pltpu.VMEM((3, 2 * frames, height + 2, width, cout), BF16),
            pltpu.VMEM((4, total + 2, height * width, 128), BF16),
            pltpu.VMEM((tm, cout, rows), BF16),
            pltpu.VMEM(side, F32),
            pltpu.VMEM(one_side, BF16),
            pltpu.VMEM(one_side, BF16),
            pltpu.VMEM(ends, BF16),
            pltpu.VMEM(ends, F32),
            pltpu.VMEM(ends, BF16),
            pltpu.SemaphoreType.DMA,
            pltpu.SemaphoreType.DMA((tm, 2)),
            pltpu.SemaphoreType.DMA((tm, 2)),
            pltpu.SemaphoreType.DMA((tm, 2)),
            pltpu.SemaphoreType.DMA((tm, 2)),
            pltpu.SemaphoreType.DMA((pairs,)),
            pltpu.SemaphoreType.DMA((pairs,)),
            pltpu.SemaphoreType.DMA((pairs, chips)),
            pltpu.SemaphoreType.DMA((pairs, chips)),
        ],
        compiler_params=pltpu.CompilerParams(
            collective_id=0, has_side_effects=True, vmem_limit_bytes=40 * 1024 * 1024
        ),
    )(
        pinned[0],
        pinned[4],
        *pinned[1:4],
    )
    results = (conv, vgrad, gw)
    conv, vgrad, gw = pl.pallas_call(
        emit,
        out_shape=tuple(jax.ShapeDtypeStruct(x.shape, x.dtype) for x in results),
        in_specs=[pl.BlockSpec(memory_space=pl.ANY)] * 3,
        out_specs=(pl.BlockSpec(memory_space=pl.ANY),) * 3,
        scratch_shapes=[pltpu.SemaphoreType.DMA((3,))],
        compiler_params=pltpu.CompilerParams(vmem_limit_bytes=1024 * 1024),
    )(*results)
    if fused:
        grad_weight = gw.T
    else:
        scale = 1.0 / math.sqrt(dp * total * height * width)
        mine = lax.psum_scatter(gw * scale, "dp", scatter_dimension=0, tiled=True)
        z = lax.axis_index("tm")
        grad_weight = lax.dynamic_slice_in_dim(mine, z * slab % cin, slab, 1).T
    return (
        conv.reshape(1, frames, height, width, cout),
        vgrad.reshape(1, frames, height, width, cin),
        grad_weight,
    )


def solution(mesh):
    in_specs = (
        P("dp", "tm", None, None, None),
        P("dp", None),
        P(),
        P(),
        P("dp", "tm", None, None, None),
    )
    out_specs = (P("dp", "tm", None, None, None), P("dp", "tm", None, None, None), P("tm", "dp"))
    sizes = (mesh.shape["tm"], mesh.shape["dp"])
    return jax.shard_map(
        functools.partial(shards, sizes), mesh=mesh, in_specs=in_specs, out_specs=out_specs, check_vma=False
    )
```

```python
import functools
import math

import jax
import jax.numpy as jnp
from jax import lax
from jax.experimental import pallas as pl
from jax.experimental.pallas import tpu as pltpu
from jax.sharding import PartitionSpec as P

MESH = pl.DeviceIdType.MESH
F32 = jnp.float32
BF16 = jnp.bfloat16


def half_roll(x):
    return pltpu.roll(x, 64, axis=1)


def shifted(x, width, b):
    if b == 1:
        return x
    rows = x.shape[0]
    column = lax.broadcasted_iota(jnp.int32, x.shape, 0) % width
    if b == 0:
        return jnp.where(column == 0, 0.0, pltpu.roll(x, 1, axis=0))
    return jnp.where(column == width - 1, 0.0, pltpu.roll(x, rows - 1, axis=0))


def kernel(
    cfg, video_ref, ids_ref, gain_ref, w_hbm, cot_ref, conv_ref, vgrad_ref, gw_ref,
    w_ref, conv_sum, grad_sum, pay, ext, cext, mask, cot_t, d32, d16, r1, s16, s32, r2,
    w_sem, send_r, send_l, recv_r, recv_l, core_send, core_recv, chip_send, chip_recv,
):
    tm, dp, frames, height, width, cin, cout, slab, pairs, fused = cfg
    total = tm * frames
    rows = frames * height * width
    pixels = height * width
    chunks = cout // 128
    z = lax.axis_index("tm")
    j = lax.axis_index("dp")
    core = j % 2
    chip = j // 2
    chips = dp // 2
    per = cout // dp

    w_copy = pltpu.make_async_copy(w_hbm, w_ref.at[pl.ds(0, 27 * cin)], w_sem)
    w_copy.start()

    barrier = pltpu.get_barrier_semaphore()

    def greet(where):
        pl.semaphore_signal(barrier, inc=1, device_id=where, device_id_type=MESH)

    @pl.when(z > 0)
    def _():
        greet((z - 1, j))

    @pl.when(z < tm - 1)
    def _():
        greet((z + 1, j))

    if fused:
        greet((z, chip * 2 + 1 - core))
        for r in range(1, chips):
            greet((z, (chip + r) % chips * 2 + core))

    video = video_ref[...].astype(F32)
    gain = gain_ref[...]
    mean_square = jnp.sum(video * video, axis=1, keepdims=True) / cin
    inv = lax.rsqrt(mean_square + 1e-06)
    normed = video * inv * gain
    sig = jax.nn.sigmoid(normed)
    act = (normed * sig).astype(BF16).astype(F32)
    lane = lax.broadcasted_iota(jnp.int32, (rows, 128), 1)
    low = lane < 64
    first = act[:, :128]
    second = jnp.concatenate([act[:, 128:], jnp.zeros((rows, 64), F32)], axis=1)
    half = rows // 2
    turned = jnp.concatenate(
        [jnp.transpose(cot_ref[:, m * 128 : (m + 1) * 128]) for m in range(chunks)], axis=0
    )
    order = [(d * 2 + e) * per for e in range(2) for d in range(chips)] if fused else [0]
    span = per if fused else cout
    for at_row, from_row in enumerate(order):
        pay[z, at_row * span : (at_row + 1) * span, :] = turned[from_row : from_row + span]
    pay[z, cout : cout + rows, :] = first.astype(BF16)
    pay[z, cout + rows :, :] = (second[:half] + half_roll(second[half:])).astype(BF16)

    peers = jnp.where(z > 0, 1, 0) + jnp.where(z < tm - 1, 1, 0)
    if fused:
        peers = peers + chips
    pl.semaphore_wait(barrier, peers)

    size = pay.shape[1] // 2

    def part_of(shard, h):
        return pay.at[shard, pl.ds(h * size, size)]

    def to_right(step, shard, h):
        return pltpu.make_async_remote_copy(
            src_ref=part_of(shard, h), dst_ref=part_of(shard, h), send_sem=send_r.at[step, h],
            recv_sem=recv_r.at[step, h], device_id=(z + 1, j), device_id_type=MESH,
        )

    def to_left(step, shard, h):
        return pltpu.make_async_remote_copy(
            src_ref=part_of(shard, h), dst_ref=part_of(shard, h), send_sem=send_l.at[step, h],
            recv_sem=recv_l.at[step, h], device_id=(z - 1, j), device_id_type=MESH,
        )

    def start_step(step, h):
        @pl.when((z < tm - 1) & (z - step >= 0))
        def _():
            to_right(step, z - step, h).start()

        @pl.when((z > 0) & (z + step <= tm - 1))
        def _():
            to_left(step, z + step, h).start()

    start_step(0, 0)
    start_step(0, 1)

    def each(start, stop, body):
        def step(n, unused):
            body(n)
            return unused

        lax.fori_loop(start, stop, step, 0)

    def clear(ref):
        def body(n):
            ref[n] = jnp.zeros(ref.shape[1:], BF16)

        each(0, ref.shape[0], body)

    clear(ext)
    clear(cext)
    clear(cot_t)
    clear(mask)
    w_ref[27 * cin :, :] = jnp.zeros((cin, cout), BF16)
    conv_sum[...] = jnp.zeros(conv_sum.shape, F32)
    grad_sum[...] = jnp.zeros(grad_sum.shape, F32)
    for t in range(total):
        for k in range(3):
            if t - 2 + k >= 0:
                same = jnp.where(ids_ref[0, t - 2 + k] == ids_ref[0, t], 1.0, 0.0)
                mask[k, t] = jnp.full((pixels, 128), same, F32).astype(BF16)

    def blocks(x):
        return x.astype(BF16).reshape(frames, height, width, 128)

    def place(shard):
        t0 = pay[shard, cout : cout + rows, :].astype(F32)
        pack = pay[shard, cout + rows :, :].astype(F32)
        plow = low[:half]
        t1 = jnp.concatenate(
            [jnp.where(plow, pack, 0.0), half_roll(jnp.where(plow, 0.0, pack))], axis=0
        )
        tiles = (
            (t0, t1),
            (half_roll(jnp.where(low, t0, 0.0)), half_roll(jnp.where(low, t1, t0))),
        )
        at = pl.ds(shard * frames + 2, frames)
        for b in range(3):
            for v in range(2):
                for n in range(2):
                    ext[v * 3 + b, at, 1 : 1 + height, :, n * 128 : (n + 1) * 128] = blocks(
                        shifted(tiles[v][n], width, b)
                    )
        cot_t[shard] = pay[shard, :cout, :]

    def place_cot(tiles, frame):
        for m in range(chunks):
            tile = tiles[m].astype(F32)
            for b in range(3):
                cext[b, frame : frame + frames, 1 : 1 + height, :, m * 128 : (m + 1) * 128] = blocks(
                    shifted(tile, width, b)
                )

    def next_tiles():
        rows_of = {at: pay[z + 1, n * span : (n + 1) * span, :] for n, at in enumerate(order)}
        natural = jnp.concatenate([rows_of[at] for at in sorted(rows_of)], axis=0)
        return [jnp.transpose(natural[m * 128 : (m + 1) * 128]) for m in range(chunks)]

    place(z)
    place_cot([cot_ref[:, m * 128 : (m + 1) * 128] for m in range(chunks)], 0)

    def pass_on(step, h):
        @pl.when(z - 1 - step >= 0)
        def _():
            to_right(step, z - 1 - step, h).wait_recv()

        @pl.when(z + 1 + step <= tm - 1)
        def _():
            to_left(step, z + 1 + step, h).wait_recv()

        if step + 1 < tm - 1:
            start_step(step + 1, h)

    def lay_out(step):
        def side(n):
            shard = z + (2 * n - 1) * (1 + step)

            @pl.when((shard >= 0) & (shard <= tm - 1))
            def _():
                place(shard)

        each(0, 2, side)
        if step == 0:
            @pl.when(z + 1 <= tm - 1)
            def _():
                place_cot(next_tiles(), frames)

    def pair_tiles(one, two, at, count):
        n = count * pixels

        def part(v, tap):
            k, a, b = tap
            block = ext[v * 3 + b, pl.ds(at + k, count), pl.ds(a, height), :, :]
            scale = mask[k, pl.ds(at, count)].reshape(n, 128)
            block = block.reshape(n, 256)
            return block[:, :128] * scale, block[:, 128:] * scale

        a0, a1 = part(0, one)
        if two is None:
            return [a0, a1[:, : cin - 128]]
        b0, b1 = part(1, two)
        return [a0, a1 + b0, b1]

    def split(tap):
        return tap // 9, tap // 3 % 3, tap % 3

    def conv_four(n):
        tap = 4 * n
        tiles = pair_tiles(split(tap), split(tap + 1), z * frames, frames)
        tiles += pair_tiles(split(tap + 2), split(tap + 3), z * frames, frames)
        at = pl.multiple_of(tap * cin, 4 * cin)
        conv_sum[...] += jnp.dot(
            jnp.concatenate(tiles, axis=1), w_ref[pl.ds(at, 4 * cin), :], preferred_element_type=F32
        )

    def grad_three(n):
        k, a = n // 3, n % 3
        scale = mask[k, pl.ds(z * frames + 2 - k, frames)].reshape(rows, 128)
        tiles, weights = [], []
        for b in range(3):
            block = cext[2 - b, pl.ds(2 - k, frames), pl.ds(2 - a, height), :, :].reshape(rows, cout)
            tiles += [block[:, m * 128 : (m + 1) * 128] * scale for m in range(chunks)]
            at = pl.multiple_of((3 * n + b) * cin, cin)
            weights.append(w_ref[pl.ds(at, cin), :])
        grad_sum[...] += lax.dot_general(
            jnp.concatenate(tiles, axis=1), jnp.concatenate(weights, axis=1),
            (((1,), (1,)), ((), ())), preferred_element_type=F32,
        )

    w_copy.wait()
    each(5, 7, conv_four)
    pass_on(0, 0)
    each(6, 9, grad_three)
    pass_on(0, 1)
    lay_out(0)
    each(0, 5, conv_four)
    conv_ref[...] = conv_sum[...].astype(BF16)
    for step in range(1, tm - 2):
        pass_on(step, 0)
        pass_on(step, 1)
        lay_out(step)

    first_tap = z * slab // cin

    def core_copy(p):
        return pltpu.make_async_remote_copy(
            src_ref=d16.at[p], dst_ref=r1.at[p], send_sem=core_send.at[p],
            recv_sem=core_recv.at[p], device_id=(z, chip * 2 + 1 - core), device_id_type=MESH,
        )

    def chip_copy(p, r):
        there = (chip + r) % chips
        return pltpu.make_async_remote_copy(
            src_ref=s16.at[p, there], dst_ref=r2.at[p, r - 1], send_sem=chip_send.at[p, r - 1],
            recv_sem=chip_recv.at[p, r - 1], device_id=(z, there * 2 + core), device_id_type=MESH,
        )

    def core_sum(p):
        core_copy(p).wait_recv()
        both = d32[p, core] + r1[p].astype(F32)
        both = both.reshape(chips, per, 2 * cin)
        s32[p] = both
        s16[p] = both.astype(BF16)
        for r in range(1, chips):
            chip_copy(p, r).start()

    def weight_part(p, cot_rows, at, count):
        one = first_tap + 2 * p
        patches = jnp.concatenate(pair_tiles(split(one), split(one + 1), at, count), axis=1)
        return jnp.dot(cot_rows, patches, preferred_element_type=F32).reshape(d32.shape[1:])

    cot_all = jnp.concatenate([cot_t[s] for s in range(tm)], axis=1)

    def early(p):
        d32[p] = weight_part(p, cot_all, 0, total)

    each(0, pairs, early)
    pass_on(tm - 2, 0)
    pass_on(tm - 2, 1)
    lay_out(tm - 2)
    last = tm - 1 - z

    def late(p):
        @pl.when((z == 0) | (z == tm - 1))
        def _():
            d32[p] = d32[p] + weight_part(p, cot_t[last], last * frames, frames)

        if fused:
            d16[p] = d32[p, 1 - core].astype(BF16)
            core_copy(p).start()

            @pl.when(p > 0)
            def _():
                core_sum(p - 1)

    each(0, pairs, late)
    if fused:
        core_sum(pairs - 1)
    else:
        for p in range(pairs):
            gw_ref[:, p * 2 * cin : (p + 1) * 2 * cin] = d32[p].reshape(cout, 2 * cin)
    each(0, 6, grad_three)
    act_grad = grad_sum[...]
    d_normed = act_grad * (sig * (1.0 + normed * (1.0 - sig))) * gain
    along = jnp.sum(d_normed * video, axis=1, keepdims=True) / cin
    vgrad_ref[...] = (inv * d_normed - video * (inv * inv * inv * along)).astype(BF16)

    if fused:
        scale = 1.0 / math.sqrt(dp * total * pixels)
        sums = []
        for p in range(pairs):
            own = s32[p, chip]
            for r in range(1, chips):
                chip_copy(p, r).wait_recv()
                own = own + r2[p, r - 1].astype(F32)
            sums.append(own * scale)
        wide = jnp.concatenate(sums, axis=1)
        skip = z * slab - first_tap * cin
        wide = pltpu.roll(wide, pairs * 2 * cin - skip, axis=1)
        gw_ref[...] = wide[:, :slab]
        for p in range(pairs):
            core_copy(p).wait_send()
            for r in range(1, chips):
                chip_copy(p, r).wait_send()

    for step in range(tm - 1):
        @pl.when((z < tm - 1) & (z - step >= 0))
        def _():
            for h in range(2):
                to_right(step, z - step, h).wait_send()

        @pl.when((z > 0) & (z + step <= tm - 1))
        def _():
            for h in range(2):
                to_left(step, z + step, h).wait_send()


def emit(*refs):
    count = len(refs) // 2
    sems = refs[-1]
    copies = [pltpu.make_async_copy(refs[n], refs[count + n], sems.at[n]) for n in range(count)]
    for copy in copies:
        copy.start()
    for copy in copies:
        copy.wait()


def shards(sizes, clip_video, clip_ids, norm_gain, conv_weight, out_cotangent):
    tm, dp = sizes
    unused, frames, height, width, cin = clip_video.shape
    krows, cout = conv_weight.shape
    rows = frames * height * width
    total = tm * frames
    slab = krows // tm
    per = cout // dp
    spans = [-(-(z * slab % cin + slab) // cin) for z in range(tm)]
    pairs = (max(spans) + 1) // 2
    fused = per % 16 == 0
    chips = dp // 2
    chunks = cout // 128
    wide = 2 * pairs * cin
    gw_shape = (per, slab) if fused else (cout, wide)
    cfg = (tm, dp, frames, height, width, cin, cout, slab, pairs, fused)
    side = (pairs, 2, cout // 2, 2 * cin)
    one_side = (pairs, cout // 2, 2 * cin) if fused else (1, 16, 128)
    ends = (pairs, chips, per, 2 * cin) if fused else (1, 1, 16, 128)
    vmem = pl.BlockSpec(memory_space=pltpu.VMEM)
    hbm = pltpu.HBM
    pinned = [
        pltpu.with_memory_space_constraint(x, hbm)
        for x in (
            clip_video.reshape(rows, cin),
            norm_gain.reshape(1, cin),
            conv_weight,
            out_cotangent.reshape(rows, cout),
            clip_ids,
        )
    ]
    conv, vgrad, gw = pl.pallas_call(
        functools.partial(kernel, cfg),
        out_shape=(
            jax.ShapeDtypeStruct((rows, cout), BF16),
            jax.ShapeDtypeStruct((rows, cin), BF16),
            jax.ShapeDtypeStruct(gw_shape, F32),
        ),
        in_specs=[vmem, pl.BlockSpec(memory_space=pltpu.SMEM), vmem, pl.BlockSpec(memory_space=pl.ANY), vmem],
        out_specs=(vmem, vmem, vmem),
        scratch_shapes=[
            pltpu.VMEM((krows + cin, cout), BF16),
            pltpu.VMEM((rows, cout), F32),
            pltpu.VMEM((rows, cin), F32),
            pltpu.VMEM((tm, (chunks + 1) * rows + rows // 2, 128), BF16),
            pltpu.VMEM((6, total + 3, height + 2, width, 256), BF16),
            pltpu.VMEM((3, 2 * frames, height + 2, width, cout), BF16),
            pltpu.VMEM((4, total + 2, height * width, 128), BF16),
            pltpu.VMEM((tm, cout, rows), BF16),
            pltpu.VMEM(side, F32),
            pltpu.VMEM(one_side, BF16),
            pltpu.VMEM(one_side, BF16),
            pltpu.VMEM(ends, BF16),
            pltpu.VMEM(ends, F32),
            pltpu.VMEM(ends, BF16),
            pltpu.SemaphoreType.DMA,
            pltpu.SemaphoreType.DMA((tm, 2)),
            pltpu.SemaphoreType.DMA((tm, 2)),
            pltpu.SemaphoreType.DMA((tm, 2)),
            pltpu.SemaphoreType.DMA((tm, 2)),
            pltpu.SemaphoreType.DMA((pairs,)),
            pltpu.SemaphoreType.DMA((pairs,)),
            pltpu.SemaphoreType.DMA((pairs, chips)),
            pltpu.SemaphoreType.DMA((pairs, chips)),
        ],
        compiler_params=pltpu.CompilerParams(
            collective_id=0, has_side_effects=True, vmem_limit_bytes=40 * 1024 * 1024
        ),
    )(
        pinned[0],
        pinned[4],
        *pinned[1:4],
    )
    results = (conv, vgrad, gw)
    conv, vgrad, gw = pl.pallas_call(
        emit,
        out_shape=tuple(jax.ShapeDtypeStruct(x.shape, x.dtype) for x in results),
        in_specs=[pl.BlockSpec(memory_space=pl.ANY)] * 3,
        out_specs=(pl.BlockSpec(memory_space=pl.ANY),) * 3,
        scratch_shapes=[pltpu.SemaphoreType.DMA((3,))],
        compiler_params=pltpu.CompilerParams(vmem_limit_bytes=1024 * 1024),
    )(*results)
    if fused:
        grad_weight = gw.T
    else:
        scale = 1.0 / math.sqrt(dp * total * height * width)
        mine = lax.psum_scatter(gw * scale, "dp", scatter_dimension=0, tiled=True)
        z = lax.axis_index("tm")
        grad_weight = lax.dynamic_slice_in_dim(mine, z * slab % cin, slab, 1).T
    return (
        conv.reshape(1, frames, height, width, cout),
        vgrad.reshape(1, frames, height, width, cin),
        grad_weight,
    )


def solution(mesh):
    in_specs = (
        P("dp", "tm", None, None, None),
        P("dp", None),
        P(),
        P(),
        P("dp", "tm", None, None, None),
    )
    out_specs = (P("dp", "tm", None, None, None), P("dp", "tm", None, None, None), P("tm", "dp"))
    sizes = (mesh.shape["tm"], mesh.shape["dp"])
    return jax.shard_map(
        functools.partial(shards, sizes), mesh=mesh, in_specs=in_specs, out_specs=out_specs, check_vma=False
    )
```

```python
import functools
import math

import jax
import jax.numpy as jnp
from jax import lax
from jax.experimental import pallas as pl
from jax.experimental.pallas import tpu as pltpu
from jax.sharding import PartitionSpec as P

MESH = pl.DeviceIdType.MESH
F32 = jnp.float32
BF16 = jnp.bfloat16


def half_roll(x):
    return pltpu.roll(x, 64, axis=1)


def shifted(x, width, b):
    if b == 1:
        return x
    rows = x.shape[0]
    column = lax.broadcasted_iota(jnp.int32, x.shape, 0) % width
    if b == 0:
        return jnp.where(column == 0, 0.0, pltpu.roll(x, 1, axis=0))
    return jnp.where(column == width - 1, 0.0, pltpu.roll(x, rows - 1, axis=0))


def kernel(
    cfg, video_ref, ids_ref, gain_ref, w_hbm, cot_ref, conv_ref, vgrad_ref, gw_ref,
    w_ref, conv_sum, grad_sum, pay, ext, cext, mask, cot_t, d32, d16, r1, s16, s32, r2,
    w_sem, send_r, send_l, recv_r, recv_l, core_send, core_recv, chip_send, chip_recv,
):
    tm, dp, frames, height, width, cin, cout, slab, pairs, fused = cfg
    total = tm * frames
    rows = frames * height * width
    pixels = height * width
    chunks = cout // 128
    z = lax.axis_index("tm")
    j = lax.axis_index("dp")
    core = j % 2
    chip = j // 2
    chips = dp // 2
    per = cout // dp

    w_copy = pltpu.make_async_copy(w_hbm, w_ref.at[pl.ds(0, 27 * cin)], w_sem)
    w_copy.start()

    barrier = pltpu.get_barrier_semaphore()

    def greet(where):
        pl.semaphore_signal(barrier, inc=1, device_id=where, device_id_type=MESH)

    short = tm == 4
    if short:
        for n in range(1, tm):
            greet(((z + n) % tm, j))
    else:
        @pl.when(z > 0)
        def _():
            greet((z - 1, j))

        @pl.when(z < tm - 1)
        def _():
            greet((z + 1, j))

    if fused:
        greet((z, chip * 2 + 1 - core))
        for r in range(1, chips):
            greet((z, (chip + r) % chips * 2 + core))

    video = video_ref[...].astype(F32)
    gain = gain_ref[...]
    mean_square = jnp.sum(video * video, axis=1, keepdims=True) / cin
    inv = lax.rsqrt(mean_square + 1e-06)
    normed = video * inv * gain
    sig = jax.nn.sigmoid(normed)
    act = (normed * sig).astype(BF16).astype(F32)
    lane = lax.broadcasted_iota(jnp.int32, (rows, 128), 1)
    low = lane < 64
    first = act[:, :128]
    second = jnp.concatenate([act[:, 128:], jnp.zeros((rows, 64), F32)], axis=1)
    half = rows // 2
    turned = jnp.concatenate(
        [jnp.transpose(cot_ref[:, m * 128 : (m + 1) * 128]) for m in range(chunks)], axis=0
    )
    order = [(d * 2 + e) * per for e in range(2) for d in range(chips)] if fused else [0]
    span = per if fused else cout
    for at_row, from_row in enumerate(order):
        pay[z, at_row * span : (at_row + 1) * span, :] = turned[from_row : from_row + span]
    pay[z, cout : cout + rows, :] = first.astype(BF16)
    pay[z, cout + rows :, :] = (second[:half] + half_roll(second[half:])).astype(BF16)

    peers = tm - 1 if short else jnp.where(z > 0, 1, 0) + jnp.where(z < tm - 1, 1, 0)
    if fused:
        peers = peers + chips
    pl.semaphore_wait(barrier, peers)

    size = pay.shape[1] // 2

    def part_of(shard, h):
        return pay.at[shard, pl.ds(h * size, size)]

    def to_right(step, shard, h):
        return pltpu.make_async_remote_copy(
            src_ref=part_of(shard, h), dst_ref=part_of(shard, h), send_sem=send_r.at[step, h],
            recv_sem=recv_r.at[step, h], device_id=(z + 1, j), device_id_type=MESH,
        )

    def to_left(step, shard, h):
        return pltpu.make_async_remote_copy(
            src_ref=part_of(shard, h), dst_ref=part_of(shard, h), send_sem=send_l.at[step, h],
            recv_sem=recv_l.at[step, h], device_id=(z - 1, j), device_id_type=MESH,
        )

    def start_step(step, h):
        @pl.when((z < tm - 1) & (z - step >= 0))
        def _():
            to_right(step, z - step, h).start()

        @pl.when((z > 0) & (z + step <= tm - 1))
        def _():
            to_left(step, z + step, h).start()

    far, near, mirror = (z + 2) % 4, z + 1 - 2 * (z % 2), 3 - z
    inner = (z == 1) | (z == 2)

    def direct(n, shard, there):
        return pltpu.make_async_remote_copy(
            src_ref=pay.at[shard], dst_ref=pay.at[shard], send_sem=send_r.at[n, 0],
            recv_sem=recv_r.at[n, 0], device_id=(there, j), device_id_type=MESH,
        )

    def relay():
        return pltpu.make_async_remote_copy(
            src_ref=pay.at[far], dst_ref=pay.at[far], send_sem=send_r.at[3, 0],
            recv_sem=recv_r.at[2, 0], device_id=(near, j), device_id_type=MESH,
        )

    if short:
        direct(0, z, far).start()
        direct(1, z, near).start()
    else:
        start_step(0, 0)
        start_step(0, 1)

    def each(start, stop, body):
        for n in range(start, stop):
            body(n)

    def loop(start, stop, body):
        def step(n, unused):
            body(n)
            return unused

        lax.fori_loop(start, stop, step, 0)

    def clear(ref):
        def body(n):
            ref[n] = jnp.zeros(ref.shape[1:], BF16)

        loop(0, ref.shape[0], body)

    clear(ext)
    clear(cext)
    clear(cot_t)
    clear(mask)
    w_ref[27 * cin :, :] = jnp.zeros((cin, cout), BF16)
    conv_sum[...] = jnp.zeros(conv_sum.shape, F32)
    grad_sum[...] = jnp.zeros(grad_sum.shape, F32)
    for t in range(total):
        for k in range(3):
            if t - 2 + k >= 0:
                same = jnp.where(ids_ref[0, t - 2 + k] == ids_ref[0, t], 1.0, 0.0)
                mask[k, t] = jnp.full((pixels, 128), same, F32).astype(BF16)

    def blocks(x):
        return x.astype(BF16).reshape(frames, height, width, 128)

    def place(shard):
        t0 = pay[shard, cout : cout + rows, :].astype(F32)
        pack = pay[shard, cout + rows :, :].astype(F32)
        plow = low[:half]
        t1 = jnp.concatenate(
            [jnp.where(plow, pack, 0.0), half_roll(jnp.where(plow, 0.0, pack))], axis=0
        )
        tiles = (
            (t0, t1),
            (half_roll(jnp.where(low, t0, 0.0)), half_roll(jnp.where(low, t1, t0))),
        )
        at = pl.ds(shard * frames + 2, frames)
        for b in range(3):
            for v in range(2):
                for n in range(2):
                    ext[v * 3 + b, at, 1 : 1 + height, :, n * 128 : (n + 1) * 128] = blocks(
                        shifted(tiles[v][n], width, b)
                    )
        cot_t[shard] = pay[shard, :cout, :]

    def place_cot(tiles, frame):
        for m in range(chunks):
            tile = tiles[m].astype(F32)
            for b in range(3):
                cext[b, frame : frame + frames, 1 : 1 + height, :, m * 128 : (m + 1) * 128] = blocks(
                    shifted(tile, width, b)
                )

    def next_tiles():
        rows_of = {at: pay[z + 1, n * span : (n + 1) * span, :] for n, at in enumerate(order)}
        natural = jnp.concatenate([rows_of[at] for at in sorted(rows_of)], axis=0)
        return [jnp.transpose(natural[m * 128 : (m + 1) * 128]) for m in range(chunks)]

    place(z)
    place_cot([cot_ref[:, m * 128 : (m + 1) * 128] for m in range(chunks)], 0)

    def pass_on(step, h):
        @pl.when(z - 1 - step >= 0)
        def _():
            to_right(step, z - 1 - step, h).wait_recv()

        @pl.when(z + 1 + step <= tm - 1)
        def _():
            to_left(step, z + 1 + step, h).wait_recv()

        if step + 1 < tm - 1:
            start_step(step + 1, h)

    def lay_out(step):
        def side(n):
            shard = z + (2 * n - 1) * (1 + step)

            @pl.when((shard >= 0) & (shard <= tm - 1))
            def _():
                place(shard)

        loop(0, 2, side)
        if step == 0:
            @pl.when(z + 1 <= tm - 1)
            def _():
                place_cot(next_tiles(), frames)

    def pair_tiles(one, two, at, count):
        n = count * pixels

        def part(v, tap):
            k, a, b = tap
            block = ext[v * 3 + b, pl.ds(at + k, count), pl.ds(a, height), :, :]
            scale = mask[k, pl.ds(at, count)].reshape(n, 128)
            block = block.reshape(n, 256)
            return block[:, :128] * scale, block[:, 128:] * scale

        a0, a1 = part(0, one)
        if two is None:
            return [a0, a1[:, : cin - 128]]
        b0, b1 = part(1, two)
        return [a0, a1 + b0, b1]

    def split(tap):
        return tap // 9, tap // 3 % 3, tap % 3

    def conv_four(n):
        tap = 4 * n
        tiles = pair_tiles(split(tap), split(tap + 1), z * frames, frames)
        tiles += pair_tiles(split(tap + 2), split(tap + 3), z * frames, frames)
        at = pl.multiple_of(tap * cin, 4 * cin)
        conv_sum[...] += jnp.dot(
            jnp.concatenate(tiles, axis=1), w_ref[pl.ds(at, 4 * cin), :], preferred_element_type=F32
        )

    def grad_three(n):
        k, a = n // 3, n % 3
        scale = mask[k, pl.ds(z * frames + 2 - k, frames)].reshape(rows, 128)
        tiles, weights = [], []
        for b in range(3):
            block = cext[2 - b, pl.ds(2 - k, frames), pl.ds(2 - a, height), :, :].reshape(rows, cout)
            tiles += [block[:, m * 128 : (m + 1) * 128] * scale for m in range(chunks)]
            at = pl.multiple_of((3 * n + b) * cin, cin)
            weights.append(w_ref[pl.ds(at, cin), :])
        grad_sum[...] += lax.dot_general(
            jnp.concatenate(tiles, axis=1), jnp.concatenate(weights, axis=1),
            (((1,), (1,)), ((), ())), preferred_element_type=F32,
        )

    def convolve():
        each(0, 5, conv_four)
        conv_ref[...] = conv_sum[...].astype(BF16)

    w_copy.wait()
    each(5, 7, conv_four)
    if not short:
        pass_on(0, 0)
    each(6, 9, grad_three)
    if short:
        direct(0, far, far).wait_recv()

        @pl.when(inner)
        def _():
            relay().start()
            direct(2, z, mirror).start()

        direct(1, near, near).wait_recv()

        def one(n):
            place(jnp.where(n == 0, far, near))

        loop(0, 2, one)

        @pl.when(z % 2 == 0)
        def _():
            place_cot(next_tiles(), frames)
    else:
        pass_on(0, 1)
        lay_out(0)
        convolve()
        for step in range(1, tm - 2):
            pass_on(step, 0)
            pass_on(step, 1)
            lay_out(step)

    first_tap = z * slab // cin

    def core_copy(p):
        return pltpu.make_async_remote_copy(
            src_ref=d16.at[p], dst_ref=r1.at[p], send_sem=core_send.at[p],
            recv_sem=core_recv.at[p], device_id=(z, chip * 2 + 1 - core), device_id_type=MESH,
        )

    def chip_copy(p, r):
        there = (chip + r) % chips
        return pltpu.make_async_remote_copy(
            src_ref=s16.at[p, there], dst_ref=r2.at[p, r - 1], send_sem=chip_send.at[p, r - 1],
            recv_sem=chip_recv.at[p, r - 1], device_id=(z, there * 2 + core), device_id_type=MESH,
        )

    def core_sum(p):
        core_copy(p).wait_recv()
        both = d32[p, core] + r1[p].astype(F32)
        both = both.reshape(chips, per, 2 * cin)
        s32[p] = both
        s16[p] = both.astype(BF16)
        for r in range(1, chips):
            chip_copy(p, r).start()

    def weight_part(p, shards_of):
        one = first_tap + 2 * p
        patches = jnp.concatenate(
            [
                jnp.concatenate(pair_tiles(split(one), split(one + 1), at * frames, count * frames), axis=1)
                for at, count in shards_of
            ],
            axis=0,
        )
        cot_rows = jnp.concatenate(
            [cot_t[at + n] for at, count in shards_of for n in range(count)], axis=1
        )
        return jnp.dot(cot_rows, patches, preferred_element_type=F32).reshape(d32.shape[1:])

    if short:
        early_runs = [(jnp.where(z == 3, 2, 0), 1), (jnp.where(z < 2, 1, 3), 1)]
        late_runs = [(jnp.where(z == 0, 2, 3 - z), 2)]
    else:
        early_runs = [(0, tm)]
        late_runs = [(tm - 1 - z, 1)]

    def early(p):
        d32[p] = weight_part(p, early_runs)

    each(0, pairs, early)
    if short:
        @pl.when(z != 2)
        def _():
            convolve()

        direct(2, mirror, mirror).wait_recv()
        place(mirror)
    else:
        pass_on(tm - 2, 0)
        pass_on(tm - 2, 1)
        lay_out(tm - 2)

    def late(p):
        def add():
            d32[p] = d32[p] + weight_part(p, late_runs)

        if short:
            add()
        else:
            pl.when((z == 0) | (z == tm - 1))(add)
        if fused:
            d16[p] = d32[p, 1 - core].astype(BF16)
            core_copy(p).start()
            if p > 0:
                core_sum(p - 1)

    each(0, pairs, late)
    if fused:
        core_sum(pairs - 1)
    else:
        for p in range(pairs):
            gw_ref[:, p * 2 * cin : (p + 1) * 2 * cin] = d32[p].reshape(cout, 2 * cin)
    if short:
        @pl.when(z == 1)
        def _():
            place_cot(next_tiles(), frames)

        @pl.when(z == 2)
        def _():
            convolve()

    each(0, 6, grad_three)
    act_grad = grad_sum[...]
    d_normed = act_grad * (sig * (1.0 + normed * (1.0 - sig))) * gain
    along = jnp.sum(d_normed * video, axis=1, keepdims=True) / cin
    vgrad_ref[...] = (inv * d_normed - video * (inv * inv * inv * along)).astype(BF16)

    if fused:
        scale = 1.0 / math.sqrt(dp * total * pixels)
        sums = []
        for p in range(pairs):
            own = s32[p, chip]
            for r in range(1, chips):
                chip_copy(p, r).wait_recv()
                own = own + r2[p, r - 1].astype(F32)
            sums.append(own * scale)
        wide = jnp.concatenate(sums, axis=1)
        skip = z * slab - first_tap * cin
        wide = pltpu.roll(wide, pairs * 2 * cin - skip, axis=1)
        gw_ref[...] = wide[:, :slab]
        for p in range(pairs):
            core_copy(p).wait_send()
            for r in range(1, chips):
                chip_copy(p, r).wait_send()

    if short:
        direct(0, z, far).wait_send()
        direct(1, z, near).wait_send()

        @pl.when(inner)
        def _():
            relay().wait_send()
            direct(2, z, mirror).wait_send()
    else:
        for step in range(tm - 1):
            @pl.when((z < tm - 1) & (z - step >= 0))
            def _():
                for h in range(2):
                    to_right(step, z - step, h).wait_send()

            @pl.when((z > 0) & (z + step <= tm - 1))
            def _():
                for h in range(2):
                    to_left(step, z + step, h).wait_send()


def emit(*refs):
    count = len(refs) // 2
    sems = refs[-1]
    copies = [pltpu.make_async_copy(refs[n], refs[count + n], sems.at[n]) for n in range(count)]
    for copy in copies:
        copy.start()
    for copy in copies:
        copy.wait()


def shards(sizes, clip_video, clip_ids, norm_gain, conv_weight, out_cotangent):
    tm, dp = sizes
    unused, frames, height, width, cin = clip_video.shape
    krows, cout = conv_weight.shape
    rows = frames * height * width
    total = tm * frames
    slab = krows // tm
    per = cout // dp
    spans = [-(-(z * slab % cin + slab) // cin) for z in range(tm)]
    pairs = (max(spans) + 1) // 2
    fused = per % 16 == 0
    chips = dp // 2
    chunks = cout // 128
    wide = 2 * pairs * cin
    gw_shape = (per, slab) if fused else (cout, wide)
    cfg = (tm, dp, frames, height, width, cin, cout, slab, pairs, fused)
    side = (pairs, 2, cout // 2, 2 * cin)
    one_side = (pairs, cout // 2, 2 * cin) if fused else (1, 16, 128)
    ends = (pairs, chips, per, 2 * cin) if fused else (1, 1, 16, 128)
    vmem = pl.BlockSpec(memory_space=pltpu.VMEM)
    hbm = pltpu.HBM
    pinned = [
        pltpu.with_memory_space_constraint(x, hbm)
        for x in (
            clip_video.reshape(rows, cin),
            norm_gain.reshape(1, cin),
            conv_weight,
            out_cotangent.reshape(rows, cout),
            clip_ids,
        )
    ]
    conv, vgrad, gw = pl.pallas_call(
        functools.partial(kernel, cfg),
        out_shape=(
            jax.ShapeDtypeStruct((rows, cout), BF16),
            jax.ShapeDtypeStruct((rows, cin), BF16),
            jax.ShapeDtypeStruct(gw_shape, F32),
        ),
        in_specs=[vmem, pl.BlockSpec(memory_space=pltpu.SMEM), vmem, pl.BlockSpec(memory_space=pl.ANY), vmem],
        out_specs=(vmem, vmem, vmem),
        scratch_shapes=[
            pltpu.VMEM((krows + cin, cout), BF16),
            pltpu.VMEM((rows, cout), F32),
            pltpu.VMEM((rows, cin), F32),
            pltpu.VMEM((tm, (chunks + 1) * rows + rows // 2, 128), BF16),
            pltpu.VMEM((6, total + 3, height + 2, width, 256), BF16),
            pltpu.VMEM((3, 2 * frames, height + 2, width, cout), BF16),
            pltpu.VMEM((4, total + 2, height * width, 128), BF16),
            pltpu.VMEM((tm, cout, rows), BF16),
            pltpu.VMEM(side, F32),
            pltpu.VMEM(one_side, BF16),
            pltpu.VMEM(one_side, BF16),
            pltpu.VMEM(ends, BF16),
            pltpu.VMEM(ends, F32),
            pltpu.VMEM(ends, BF16),
            pltpu.SemaphoreType.DMA,
            pltpu.SemaphoreType.DMA((tm, 2)),
            pltpu.SemaphoreType.DMA((tm, 2)),
            pltpu.SemaphoreType.DMA((tm, 2)),
            pltpu.SemaphoreType.DMA((tm, 2)),
            pltpu.SemaphoreType.DMA((pairs,)),
            pltpu.SemaphoreType.DMA((pairs,)),
            pltpu.SemaphoreType.DMA((pairs, chips)),
            pltpu.SemaphoreType.DMA((pairs, chips)),
        ],
        compiler_params=pltpu.CompilerParams(
            collective_id=0, has_side_effects=True, vmem_limit_bytes=40 * 1024 * 1024
        ),
    )(
        pinned[0],
        pinned[4],
        *pinned[1:4],
    )
    results = (conv, vgrad, gw)
    conv, vgrad, gw = pl.pallas_call(
        emit,
        out_shape=tuple(jax.ShapeDtypeStruct(x.shape, x.dtype) for x in results),
        in_specs=[pl.BlockSpec(memory_space=pl.ANY)] * 3,
        out_specs=(pl.BlockSpec(memory_space=pl.ANY),) * 3,
        scratch_shapes=[pltpu.SemaphoreType.DMA((3,))],
        compiler_params=pltpu.CompilerParams(vmem_limit_bytes=1024 * 1024),
    )(*results)
    if fused:
        grad_weight = gw.T
    else:
        scale = 1.0 / math.sqrt(dp * total * height * width)
        mine = lax.psum_scatter(gw * scale, "dp", scatter_dimension=0, tiled=True)
        z = lax.axis_index("tm")
        grad_weight = lax.dynamic_slice_in_dim(mine, z * slab % cin, slab, 1).T
    return (
        conv.reshape(1, frames, height, width, cout),
        vgrad.reshape(1, frames, height, width, cin),
        grad_weight,
    )


def solution(mesh):
    in_specs = (
        P("dp", "tm", None, None, None),
        P("dp", None),
        P(),
        P(),
        P("dp", "tm", None, None, None),
    )
    out_specs = (P("dp", "tm", None, None, None), P("dp", "tm", None, None, None), P("tm", "dp"))
    sizes = (mesh.shape["tm"], mesh.shape["dp"])
    return jax.shard_map(
        functools.partial(shards, sizes), mesh=mesh, in_specs=in_specs, out_specs=out_specs, check_vma=False
    )
```

```python
import functools
import math

import jax
import jax.numpy as jnp
from jax import lax
from jax.experimental import pallas as pl
from jax.experimental.pallas import tpu as pltpu
from jax.sharding import PartitionSpec as P

MESH = pl.DeviceIdType.MESH
F32 = jnp.float32
BF16 = jnp.bfloat16


def half_roll(x):
    return pltpu.roll(x, 64, axis=1)


def shifted(x, width, b):
    if b == 1:
        return x
    rows = x.shape[0]
    column = lax.broadcasted_iota(jnp.int32, x.shape, 0) % width
    if b == 0:
        return jnp.where(column == 0, 0.0, pltpu.roll(x, 1, axis=0))
    return jnp.where(column == width - 1, 0.0, pltpu.roll(x, rows - 1, axis=0))


def kernel(
    cfg, video_ref, ids_ref, gain_ref, w_hbm, cot_ref, conv_ref, vgrad_ref, gw_ref,
    w_ref, conv_sum, grad_sum, pay, ext, cext, mask, cot_t, d32, d16, r1, s16, s32, r2,
    w_sem, send_r, send_l, recv_r, recv_l, core_send, core_recv, chip_send, chip_recv,
):
    tm, dp, frames, height, width, cin, cout, slab, pairs, fused = cfg
    total = tm * frames
    rows = frames * height * width
    pixels = height * width
    chunks = cout // 128
    z = lax.axis_index("tm")
    j = lax.axis_index("dp")
    core = j % 2
    chip = j // 2
    chips = dp // 2
    per = cout // dp

    w_copy = pltpu.make_async_copy(w_hbm, w_ref.at[pl.ds(0, 27 * cin)], w_sem)
    w_copy.start()

    barrier = pltpu.get_barrier_semaphore()

    def greet(where):
        pl.semaphore_signal(barrier, inc=1, device_id=where, device_id_type=MESH)

    short = tm == 4
    if short:
        for n in range(1, tm):
            greet(((z + n) % tm, j))
    else:
        @pl.when(z > 0)
        def _():
            greet((z - 1, j))

        @pl.when(z < tm - 1)
        def _():
            greet((z + 1, j))

    if fused:
        greet((z, chip * 2 + 1 - core))
        for r in range(1, chips):
            greet((z, (chip + r) % chips * 2 + core))

    video = video_ref[...].astype(F32)
    gain = gain_ref[...]
    mean_square = jnp.sum(video * video, axis=1, keepdims=True) / cin
    inv = lax.rsqrt(mean_square + 1e-06)
    normed = video * inv * gain
    sig = jax.nn.sigmoid(normed)
    act = (normed * sig).astype(BF16).astype(F32)
    lane = lax.broadcasted_iota(jnp.int32, (rows, 128), 1)
    low = lane < 64
    first = act[:, :128]
    second = jnp.concatenate([act[:, 128:], jnp.zeros((rows, 64), F32)], axis=1)
    half = rows // 2
    turned = jnp.concatenate(
        [jnp.transpose(cot_ref[:, m * 128 : (m + 1) * 128]) for m in range(chunks)], axis=0
    )
    order = [(d * 2 + e) * per for e in range(2) for d in range(chips)] if fused else [0]
    span = per if fused else cout
    for at_row, from_row in enumerate(order):
        pay[z, at_row * span : (at_row + 1) * span, :] = turned[from_row : from_row + span]
    pay[z, cout : cout + rows, :] = first.astype(BF16)
    pay[z, cout + rows :, :] = (second[:half] + half_roll(second[half:])).astype(BF16)

    peers = tm - 1 if short else jnp.where(z > 0, 1, 0) + jnp.where(z < tm - 1, 1, 0)
    if fused:
        peers = peers + chips
    pl.semaphore_wait(barrier, peers)

    size = pay.shape[1] // 2

    def part_of(shard, h):
        return pay.at[shard, pl.ds(h * size, size)]

    def to_right(step, shard, h):
        return pltpu.make_async_remote_copy(
            src_ref=part_of(shard, h), dst_ref=part_of(shard, h), send_sem=send_r.at[step, h],
            recv_sem=recv_r.at[step, h], device_id=(z + 1, j), device_id_type=MESH,
        )

    def to_left(step, shard, h):
        return pltpu.make_async_remote_copy(
            src_ref=part_of(shard, h), dst_ref=part_of(shard, h), send_sem=send_l.at[step, h],
            recv_sem=recv_l.at[step, h], device_id=(z - 1, j), device_id_type=MESH,
        )

    def start_step(step, h):
        @pl.when((z < tm - 1) & (z - step >= 0))
        def _():
            to_right(step, z - step, h).start()

        @pl.when((z > 0) & (z + step <= tm - 1))
        def _():
            to_left(step, z + step, h).start()

    far, near, mirror = (z + 2) % 4, z + 1 - 2 * (z % 2), 3 - z
    inner = (z == 1) | (z == 2)

    def direct(n, shard, there):
        return pltpu.make_async_remote_copy(
            src_ref=pay.at[shard], dst_ref=pay.at[shard], send_sem=send_r.at[n, 0],
            recv_sem=recv_r.at[n, 0], device_id=(there, j), device_id_type=MESH,
        )

    def relay():
        return pltpu.make_async_remote_copy(
            src_ref=pay.at[far], dst_ref=pay.at[far], send_sem=send_r.at[3, 0],
            recv_sem=recv_r.at[2, 0], device_id=(near, j), device_id_type=MESH,
        )

    if short:
        direct(0, z, far).start()
        direct(1, z, near).start()
    else:
        start_step(0, 0)
        start_step(0, 1)

    def each(start, stop, body):
        for n in range(start, stop):
            body(n)

    def loop(start, stop, body):
        def step(n, unused):
            body(n)
            return unused

        lax.fori_loop(start, stop, step, 0)

    def clear(ref):
        def body(n):
            ref[n] = jnp.zeros(ref.shape[1:], BF16)

        loop(0, ref.shape[0], body)

    clear(ext)
    clear(cext)
    clear(cot_t)
    clear(mask)
    w_ref[27 * cin :, :] = jnp.zeros((cin, cout), BF16)
    conv_sum[...] = jnp.zeros(conv_sum.shape, F32)
    grad_sum[...] = jnp.zeros(grad_sum.shape, F32)
    for t in range(total):
        for k in range(3):
            if t - 2 + k >= 0:
                same = jnp.where(ids_ref[0, t - 2 + k] == ids_ref[0, t], 1.0, 0.0)
                mask[k, t] = jnp.full((pixels, 128), same, F32).astype(BF16)

    def blocks(x):
        return x.astype(BF16).reshape(frames, height, width, 128)

    def place(shard):
        t0 = pay[shard, cout : cout + rows, :].astype(F32)
        pack = pay[shard, cout + rows :, :].astype(F32)
        plow = low[:half]
        t1 = jnp.concatenate(
            [jnp.where(plow, pack, 0.0), half_roll(jnp.where(plow, 0.0, pack))], axis=0
        )
        tiles = (
            (t0, t1),
            (half_roll(jnp.where(low, t0, 0.0)), half_roll(jnp.where(low, t1, t0))),
        )
        at = pl.ds(shard * frames + 2, frames)
        for b in range(3):
            for v in range(2):
                for n in range(2):
                    ext[v * 3 + b, at, 1 : 1 + height, :, n * 128 : (n + 1) * 128] = blocks(
                        shifted(tiles[v][n], width, b)
                    )
        cot_t[shard] = pay[shard, :cout, :]

    def place_cot(tiles, frame):
        for m in range(chunks):
            tile = tiles[m].astype(F32)
            for b in range(3):
                cext[b, frame : frame + frames, 1 : 1 + height, :, m * 128 : (m + 1) * 128] = blocks(
                    shifted(tile, width, b)
                )

    def next_tiles():
        rows_of = {at: pay[z + 1, n * span : (n + 1) * span, :] for n, at in enumerate(order)}
        natural = jnp.concatenate([rows_of[at] for at in sorted(rows_of)], axis=0)
        return [jnp.transpose(natural[m * 128 : (m + 1) * 128]) for m in range(chunks)]

    place(z)
    place_cot([cot_ref[:, m * 128 : (m + 1) * 128] for m in range(chunks)], 0)

    def pass_on(step, h):
        @pl.when(z - 1 - step >= 0)
        def _():
            to_right(step, z - 1 - step, h).wait_recv()

        @pl.when(z + 1 + step <= tm - 1)
        def _():
            to_left(step, z + 1 + step, h).wait_recv()

        if step + 1 < tm - 1:
            start_step(step + 1, h)

    def lay_out(step):
        def side(n):
            shard = z + (2 * n - 1) * (1 + step)

            @pl.when((shard >= 0) & (shard <= tm - 1))
            def _():
                place(shard)

        loop(0, 2, side)
        if step == 0:
            @pl.when(z + 1 <= tm - 1)
            def _():
                place_cot(next_tiles(), frames)

    def pair_tiles(one, two, at, count):
        n = count * pixels

        def part(v, tap):
            k, a, b = tap
            block = ext[v * 3 + b, pl.ds(at + k, count), pl.ds(a, height), :, :]
            scale = mask[k, pl.ds(at, count)].reshape(n, 128)
            block = block.reshape(n, 256)
            return block[:, :128] * scale, block[:, 128:] * scale

        a0, a1 = part(0, one)
        if two is None:
            return [a0, a1[:, : cin - 128]]
        b0, b1 = part(1, two)
        return [a0, a1 + b0, b1]

    def split(tap):
        return tap // 9, tap // 3 % 3, tap % 3

    def conv_four(n):
        tap = 4 * n
        tiles = pair_tiles(split(tap), split(tap + 1), z * frames, frames)
        tiles += pair_tiles(split(tap + 2), split(tap + 3), z * frames, frames)
        at = pl.multiple_of(tap * cin, 4 * cin)
        conv_sum[...] += jnp.dot(
            jnp.concatenate(tiles, axis=1), w_ref[pl.ds(at, 4 * cin), :], preferred_element_type=F32
        )

    def grad_three(n):
        k, a = n // 3, n % 3
        scale = mask[k, pl.ds(z * frames + 2 - k, frames)].reshape(rows, 128)
        tiles, weights = [], []
        for b in range(3):
            block = cext[2 - b, pl.ds(2 - k, frames), pl.ds(2 - a, height), :, :].reshape(rows, cout)
            tiles += [block[:, m * 128 : (m + 1) * 128] * scale for m in range(chunks)]
            at = pl.multiple_of((3 * n + b) * cin, cin)
            weights.append(w_ref[pl.ds(at, cin), :])
        grad_sum[...] += lax.dot_general(
            jnp.concatenate(tiles, axis=1), jnp.concatenate(weights, axis=1),
            (((1,), (1,)), ((), ())), preferred_element_type=F32,
        )

    def convolve():
        each(0, 5, conv_four)
        conv_ref[...] = conv_sum[...].astype(BF16)

    w_copy.wait()
    each(5, 7, conv_four)
    if not short:
        pass_on(0, 0)
    each(6, 9, grad_three)
    if short:
        direct(0, far, far).wait_recv()

        @pl.when(inner)
        def _():
            relay().start()
            direct(2, z, mirror).start()

        direct(1, near, near).wait_recv()

        def one(n):
            place(jnp.where(n == 0, far, near))

        loop(0, 2, one)

        @pl.when(z % 2 == 0)
        def _():
            place_cot(next_tiles(), frames)
    else:
        pass_on(0, 1)
        lay_out(0)
        convolve()
        for step in range(1, tm - 2):
            pass_on(step, 0)
            pass_on(step, 1)
            lay_out(step)

    first_tap = z * slab // cin

    def core_copy(p):
        return pltpu.make_async_remote_copy(
            src_ref=d16.at[p], dst_ref=r1.at[p], send_sem=core_send.at[p],
            recv_sem=core_recv.at[p], device_id=(z, chip * 2 + 1 - core), device_id_type=MESH,
        )

    def chip_copy(p, r):
        there = (chip + r) % chips
        return pltpu.make_async_remote_copy(
            src_ref=s16.at[p, there], dst_ref=r2.at[p, r - 1], send_sem=chip_send.at[p, r - 1],
            recv_sem=chip_recv.at[p, r - 1], device_id=(z, there * 2 + core), device_id_type=MESH,
        )

    def core_sum(p):
        core_copy(p).wait_recv()
        both = d32[p, core] + r1[p].astype(F32)
        both = both.reshape(chips, per, 2 * cin)
        s32[p] = both
        s16[p] = both.astype(BF16)
        for r in range(1, chips):
            chip_copy(p, r).start()

    def weight_part(p, shards_of):
        one = first_tap + 2 * p
        patches = jnp.concatenate(
            [
                jnp.concatenate(pair_tiles(split(one), split(one + 1), at * frames, count * frames), axis=1)
                for at, count in shards_of
            ],
            axis=0,
        )
        cot_rows = jnp.concatenate(
            [cot_t[at + n] for at, count in shards_of for n in range(count)], axis=1
        )
        return jnp.dot(cot_rows, patches, preferred_element_type=F32).reshape(d32.shape[1:])

    if short:
        early_runs = [(jnp.where(z == 3, 2, 0), 1), (jnp.where(z < 2, 1, 3), 1)]
        late_runs = [(jnp.where(z == 0, 2, 3 - z), 2)]
    else:
        early_runs = [(0, tm)]
        late_runs = [(tm - 1 - z, 1)]

    def early(p):
        d32[p] = weight_part(p, early_runs)

    each(0, pairs, early)
    if short:
        @pl.when(z != 2)
        def _():
            convolve()

        @pl.when(z != 1)
        def _():
            each(0, 4, grad_three)

        direct(2, mirror, mirror).wait_recv()
        place(mirror)
    else:
        pass_on(tm - 2, 0)
        pass_on(tm - 2, 1)
        lay_out(tm - 2)

    def late(p):
        def add():
            d32[p] = d32[p] + weight_part(p, late_runs)

        if short:
            add()
        else:
            pl.when((z == 0) | (z == tm - 1))(add)
        if fused:
            d16[p] = d32[p, 1 - core].astype(BF16)
            core_copy(p).start()
            if p > 0:
                core_sum(p - 1)

    each(0, pairs, late)
    if fused:
        core_sum(pairs - 1)
    else:
        for p in range(pairs):
            gw_ref[:, p * 2 * cin : (p + 1) * 2 * cin] = d32[p].reshape(cout, 2 * cin)
    if short:
        @pl.when(z == 1)
        def _():
            place_cot(next_tiles(), frames)
            each(0, 4, grad_three)

        @pl.when(z == 2)
        def _():
            convolve()

    each(4 if short else 0, 6, grad_three)
    act_grad = grad_sum[...]
    d_normed = act_grad * (sig * (1.0 + normed * (1.0 - sig))) * gain
    along = jnp.sum(d_normed * video, axis=1, keepdims=True) / cin
    vgrad_ref[...] = (inv * d_normed - video * (inv * inv * inv * along)).astype(BF16)

    if fused:
        scale = 1.0 / math.sqrt(dp * total * pixels)
        sums = []
        for p in range(pairs):
            own = s32[p, chip]
            for r in range(1, chips):
                chip_copy(p, r).wait_recv()
                own = own + r2[p, r - 1].astype(F32)
            sums.append(own * scale)
        wide = jnp.concatenate(sums, axis=1)
        skip = z * slab - first_tap * cin
        wide = pltpu.roll(wide, pairs * 2 * cin - skip, axis=1)
        gw_ref[...] = wide[:, :slab]
        for p in range(pairs):
            core_copy(p).wait_send()
            for r in range(1, chips):
                chip_copy(p, r).wait_send()

    if short:
        direct(0, z, far).wait_send()
        direct(1, z, near).wait_send()

        @pl.when(inner)
        def _():
            relay().wait_send()
            direct(2, z, mirror).wait_send()
    else:
        for step in range(tm - 1):
            @pl.when((z < tm - 1) & (z - step >= 0))
            def _():
                for h in range(2):
                    to_right(step, z - step, h).wait_send()

            @pl.when((z > 0) & (z + step <= tm - 1))
            def _():
                for h in range(2):
                    to_left(step, z + step, h).wait_send()


def emit(*refs):
    count = len(refs) // 2
    sems = refs[-1]
    copies = [pltpu.make_async_copy(refs[n], refs[count + n], sems.at[n]) for n in range(count)]
    for copy in copies:
        copy.start()
    for copy in copies:
        copy.wait()


def shards(sizes, clip_video, clip_ids, norm_gain, conv_weight, out_cotangent):
    tm, dp = sizes
    unused, frames, height, width, cin = clip_video.shape
    krows, cout = conv_weight.shape
    rows = frames * height * width
    total = tm * frames
    slab = krows // tm
    per = cout // dp
    spans = [-(-(z * slab % cin + slab) // cin) for z in range(tm)]
    pairs = (max(spans) + 1) // 2
    fused = per % 16 == 0
    chips = dp // 2
    chunks = cout // 128
    wide = 2 * pairs * cin
    gw_shape = (per, slab) if fused else (cout, wide)
    cfg = (tm, dp, frames, height, width, cin, cout, slab, pairs, fused)
    side = (pairs, 2, cout // 2, 2 * cin)
    one_side = (pairs, cout // 2, 2 * cin) if fused else (1, 16, 128)
    ends = (pairs, chips, per, 2 * cin) if fused else (1, 1, 16, 128)
    vmem = pl.BlockSpec(memory_space=pltpu.VMEM)
    hbm = pltpu.HBM
    pinned = [
        pltpu.with_memory_space_constraint(x, hbm)
        for x in (
            clip_video.reshape(rows, cin),
            norm_gain.reshape(1, cin),
            conv_weight,
            out_cotangent.reshape(rows, cout),
            clip_ids,
        )
    ]
    conv, vgrad, gw = pl.pallas_call(
        functools.partial(kernel, cfg),
        out_shape=(
            jax.ShapeDtypeStruct((rows, cout), BF16),
            jax.ShapeDtypeStruct((rows, cin), BF16),
            jax.ShapeDtypeStruct(gw_shape, F32),
        ),
        in_specs=[vmem, pl.BlockSpec(memory_space=pltpu.SMEM), vmem, pl.BlockSpec(memory_space=pl.ANY), vmem],
        out_specs=(vmem, vmem, vmem),
        scratch_shapes=[
            pltpu.VMEM((krows + cin, cout), BF16),
            pltpu.VMEM((rows, cout), F32),
            pltpu.VMEM((rows, cin), F32),
            pltpu.VMEM((tm, (chunks + 1) * rows + rows // 2, 128), BF16),
            pltpu.VMEM((6, total + 3, height + 2, width, 256), BF16),
            pltpu.VMEM((3, 2 * frames, height + 2, width, cout), BF16),
            pltpu.VMEM((4, total + 2, height * width, 128), BF16),
            pltpu.VMEM((tm, cout, rows), BF16),
            pltpu.VMEM(side, F32),
            pltpu.VMEM(one_side, BF16),
            pltpu.VMEM(one_side, BF16),
            pltpu.VMEM(ends, BF16),
            pltpu.VMEM(ends, F32),
            pltpu.VMEM(ends, BF16),
            pltpu.SemaphoreType.DMA,
            pltpu.SemaphoreType.DMA((tm, 2)),
            pltpu.SemaphoreType.DMA((tm, 2)),
            pltpu.SemaphoreType.DMA((tm, 2)),
            pltpu.SemaphoreType.DMA((tm, 2)),
            pltpu.SemaphoreType.DMA((pairs,)),
            pltpu.SemaphoreType.DMA((pairs,)),
            pltpu.SemaphoreType.DMA((pairs, chips)),
            pltpu.SemaphoreType.DMA((pairs, chips)),
        ],
        compiler_params=pltpu.CompilerParams(
            collective_id=0, has_side_effects=True, vmem_limit_bytes=40 * 1024 * 1024
        ),
    )(
        pinned[0],
        pinned[4],
        *pinned[1:4],
    )
    results = (conv, vgrad, gw)
    conv, vgrad, gw = pl.pallas_call(
        emit,
        out_shape=tuple(jax.ShapeDtypeStruct(x.shape, x.dtype) for x in results),
        in_specs=[pl.BlockSpec(memory_space=pl.ANY)] * 3,
        out_specs=(pl.BlockSpec(memory_space=pl.ANY),) * 3,
        scratch_shapes=[pltpu.SemaphoreType.DMA((3,))],
        compiler_params=pltpu.CompilerParams(vmem_limit_bytes=1024 * 1024),
    )(*results)
    if fused:
        grad_weight = gw.T
    else:
        scale = 1.0 / math.sqrt(dp * total * height * width)
        mine = lax.psum_scatter(gw * scale, "dp", scatter_dimension=0, tiled=True)
        z = lax.axis_index("tm")
        grad_weight = lax.dynamic_slice_in_dim(mine, z * slab % cin, slab, 1).T
    return (
        conv.reshape(1, frames, height, width, cout),
        vgrad.reshape(1, frames, height, width, cin),
        grad_weight,
    )


def solution(mesh):
    in_specs = (
        P("dp", "tm", None, None, None),
        P("dp", None),
        P(),
        P(),
        P("dp", "tm", None, None, None),
    )
    out_specs = (P("dp", "tm", None, None, None), P("dp", "tm", None, None, None), P("tm", "dp"))
    sizes = (mesh.shape["tm"], mesh.shape["dp"])
    return jax.shard_map(
        functools.partial(shards, sizes), mesh=mesh, in_specs=in_specs, out_specs=out_specs, check_vma=False
    )
```

```python
import functools
import math

import jax
import jax.numpy as jnp
from jax import lax
from jax.experimental import pallas as pl
from jax.experimental.pallas import tpu as pltpu
from jax.sharding import PartitionSpec as P

MESH = pl.DeviceIdType.MESH
F32 = jnp.float32
BF16 = jnp.bfloat16


def half_roll(x):
    return pltpu.roll(x, 64, axis=1)


def shifted(x, width, b):
    if b == 1:
        return x
    rows = x.shape[0]
    column = lax.broadcasted_iota(jnp.int32, x.shape, 0) % width
    if b == 0:
        return jnp.where(column == 0, 0.0, pltpu.roll(x, 1, axis=0))
    return jnp.where(column == width - 1, 0.0, pltpu.roll(x, rows - 1, axis=0))


def kernel(
    cfg, video_ref, ids_ref, gain_ref, w_hbm, cot_ref, conv_ref, vgrad_ref, gw_ref,
    w_ref, pay, ext, cext, mask, cot_t, d32, d16, r1, s16, s32, r2,
    w_sem, send_r, send_l, recv_r, recv_l, core_send, core_recv, chip_send, chip_recv,
):
    tm, dp, frames, height, width, cin, cout, slab, pairs, fused = cfg
    total = tm * frames
    rows = frames * height * width
    pixels = height * width
    chunks = cout // 128
    z = lax.axis_index("tm")
    j = lax.axis_index("dp")
    core = j % 2
    chip = j // 2
    chips = dp // 2
    per = cout // dp

    w_copy = pltpu.make_async_copy(w_hbm, w_ref, w_sem)
    w_copy.start()

    barrier = pltpu.get_barrier_semaphore()

    def greet(where):
        pl.semaphore_signal(barrier, inc=1, device_id=where, device_id_type=MESH)

    @pl.when(z > 0)
    def _():
        greet((z - 1, j))

    @pl.when(z < tm - 1)
    def _():
        greet((z + 1, j))

    if fused:
        greet((z, chip * 2 + 1 - core))
        for r in range(1, chips):
            greet((z, (chip + r) % chips * 2 + core))

    video = video_ref[...].astype(F32)
    gain = gain_ref[...]
    mean_square = jnp.sum(video * video, axis=1, keepdims=True) / cin
    inv = lax.rsqrt(mean_square + 1e-06)
    normed = video * inv * gain
    sig = jax.nn.sigmoid(normed)
    act = (normed * sig).astype(BF16).astype(F32)
    lane = lax.broadcasted_iota(jnp.int32, (rows, 128), 1)
    low = lane < 64
    first = act[:, :128]
    second = jnp.concatenate([act[:, 128:], jnp.zeros((rows, 64), F32)], axis=1)
    half = rows // 2
    turned = jnp.concatenate(
        [jnp.transpose(cot_ref[:, m * 128 : (m + 1) * 128]) for m in range(chunks)], axis=0
    )
    order = [(d * 2 + e) * per for e in range(2) for d in range(chips)] if fused else [0]
    span = per if fused else cout
    for at_row, from_row in enumerate(order):
        pay[z, at_row * span : (at_row + 1) * span, :] = turned[from_row : from_row + span]
    pay[z, cout : cout + rows, :] = first.astype(BF16)
    pay[z, cout + rows :, :] = (second[:half] + half_roll(second[half:])).astype(BF16)

    peers = jnp.where(z > 0, 1, 0) + jnp.where(z < tm - 1, 1, 0)
    if fused:
        peers = peers + chips
    pl.semaphore_wait(barrier, peers)

    size = pay.shape[1] // 2

    def part_of(shard, h):
        return pay.at[shard, pl.ds(h * size, size)]

    def to_right(step, shard, h):
        return pltpu.make_async_remote_copy(
            src_ref=part_of(shard, h), dst_ref=part_of(shard, h), send_sem=send_r.at[step, h],
            recv_sem=recv_r.at[step, h], device_id=(z + 1, j), device_id_type=MESH,
        )

    def to_left(step, shard, h):
        return pltpu.make_async_remote_copy(
            src_ref=part_of(shard, h), dst_ref=part_of(shard, h), send_sem=send_l.at[step, h],
            recv_sem=recv_l.at[step, h], device_id=(z - 1, j), device_id_type=MESH,
        )

    def start_step(step, h):
        @pl.when((z < tm - 1) & (z - step >= 0))
        def _():
            to_right(step, z - step, h).start()

        @pl.when((z > 0) & (z + step <= tm - 1))
        def _():
            to_left(step, z + step, h).start()

    start_step(0, 0)
    start_step(0, 1)

    ext[...] = jnp.zeros(ext.shape, BF16)
    cext[...] = jnp.zeros(cext.shape, BF16)
    cot_t[...] = jnp.zeros(cot_t.shape, BF16)
    mask[...] = jnp.zeros(mask.shape, BF16)
    for t in range(total):
        for k in range(3):
            if t - 2 + k >= 0:
                same = jnp.where(ids_ref[0, t - 2 + k] == ids_ref[0, t], 1.0, 0.0)
                mask[k, t] = jnp.full((pixels, 128), same, F32).astype(BF16)

    def blocks(x):
        return x.astype(BF16).reshape(frames, height, width, 128)

    def place(shard):
        t0 = pay[shard, cout : cout + rows, :].astype(F32)
        pack = pay[shard, cout + rows :, :].astype(F32)
        plow = low[:half]
        t1 = jnp.concatenate(
            [jnp.where(plow, pack, 0.0), half_roll(jnp.where(plow, 0.0, pack))], axis=0
        )
        tiles = (
            (t0, t1),
            (half_roll(jnp.where(low, t0, 0.0)), half_roll(jnp.where(low, t1, t0))),
        )
        at = pl.ds(shard * frames + 2, frames)
        for b in range(3):
            for v in range(2):
                for n in range(2):
                    ext[v, b, at, 1 : 1 + height, :, n * 128 : (n + 1) * 128] = blocks(
                        shifted(tiles[v][n], width, b)
                    )
        cot_t[shard] = pay[shard, :cout, :]

    def place_cot(tiles, frame):
        for m in range(chunks):
            tile = tiles[m].astype(F32)
            for b in range(3):
                cext[b, frame : frame + frames, 1 : 1 + height, :, m * 128 : (m + 1) * 128] = blocks(
                    shifted(tile, width, b)
                )

    def next_tiles():
        rows_of = {at: pay[z + 1, n * span : (n + 1) * span, :] for n, at in enumerate(order)}
        natural = jnp.concatenate([rows_of[at] for at in sorted(rows_of)], axis=0)
        return [jnp.transpose(natural[m * 128 : (m + 1) * 128]) for m in range(chunks)]

    place(z)
    place_cot([cot_ref[:, m * 128 : (m + 1) * 128] for m in range(chunks)], 0)

    def pass_on(step, h):
        @pl.when(z - 1 - step >= 0)
        def _():
            to_right(step, z - 1 - step, h).wait_recv()

        @pl.when(z + 1 + step <= tm - 1)
        def _():
            to_left(step, z + 1 + step, h).wait_recv()

        if step + 1 < tm - 1:
            start_step(step + 1, h)

    def lay_out(step):
        @pl.when(z - 1 - step >= 0)
        def _():
            place(z - 1 - step)

        @pl.when(z + 1 + step <= tm - 1)
        def _():
            place(z + 1 + step)
            if step == 0:
                place_cot(next_tiles(), frames)

    def pair_tiles(one, two, at, count):
        n = count * pixels

        def part(v, tap):
            k, a, b = tap
            block = ext[v, b, pl.ds(at + k, count), pl.ds(a, height), :, :]
            scale = mask[k, pl.ds(at, count)].reshape(n, 128)
            block = block.reshape(n, 256)
            return block[:, :128] * scale, block[:, 128:] * scale

        a0, a1 = part(0, one)
        if two is None:
            return [a0, a1[:, : cin - 128]]
        b0, b1 = part(1, two)
        return [a0, a1 + b0, b1]

    def conv_some(taps):
        tiles = []
        for n in range(0, len(taps), 2):
            two = taps[n + 1] if n + 1 < len(taps) else None
            tiles += pair_tiles(split(taps[n]), None if two is None else split(two), z * frames, frames)
        return jnp.dot(
            jnp.concatenate(tiles, axis=1),
            w_ref[taps[0] * cin : (taps[-1] + 1) * cin, :],
            preferred_element_type=F32,
        )

    def split(tap):
        return tap // 9, tap // 3 % 3, tap % 3

    def conv_range(start, stop):
        found = jnp.zeros((rows, cout), F32)
        for n in range(start, stop, 4):
            found = found + conv_some(list(range(n, min(n + 4, stop))))
        return found

    def grad_range(start, stop):
        found = jnp.zeros((rows, cin), F32)

        def columns(tap):
            k, a, b = split(tap)
            block = cext[2 - b, 2 - k : 2 - k + frames, 2 - a : 2 - a + height, :, :].reshape(rows, cout)
            if k == 2:
                return [block]
            scale = mask[k, pl.ds(z * frames + 2 - k, frames)].reshape(rows, 128)
            return [block[:, m * 128 : (m + 1) * 128] * scale for m in range(chunks)]

        for first in range(start, stop, 2):
            taps = range(first, min(first + 2, stop))
            found = found + lax.dot_general(
                jnp.concatenate([tile for tap in taps for tile in columns(tap)], axis=1),
                jnp.concatenate([w_ref[tap * cin : (tap + 1) * cin, :] for tap in taps], axis=1),
                (((1,), (1,)), ((), ())),
                preferred_element_type=F32,
            )
        return found

    w_copy.wait()
    conv = conv_range(18, 27)
    pass_on(0, 0)
    act_grad = grad_range(18, 24)
    pass_on(0, 1)
    lay_out(0)
    conv = conv + conv_range(0, 8)
    if tm > 3:
        pass_on(1, 0)
    conv = conv + conv_range(8, 16)
    for step in range(1, tm - 2):
        if step > 1:
            pass_on(step, 0)
        pass_on(step, 1)
        lay_out(step)
    conv_ref[...] = (conv + conv_range(16, 18)).astype(BF16)

    first_tap = z * slab // cin

    def core_copy(p):
        return pltpu.make_async_remote_copy(
            src_ref=d16.at[p], dst_ref=r1.at[p], send_sem=core_send.at[p],
            recv_sem=core_recv.at[p], device_id=(z, chip * 2 + 1 - core), device_id_type=MESH,
        )

    skip = z * slab - first_tap * cin

    def for_lanes(p, do):
        if p == 0:
            narrow, lanes = skip >= 128, (128, 2 * cin - 128)
        elif p == pairs - 1:
            narrow, lanes = skip + slab <= p * 2 * cin + 256, (0, 256)
        else:
            do((0, 2 * cin))
            return

        @pl.when(narrow)
        def _():
            do(lanes)

        @pl.when(jnp.logical_not(narrow))
        def _():
            do((0, 2 * cin))

    def chip_copy(p, r, lanes):
        there = (chip + r) % chips
        return pltpu.make_async_remote_copy(
            src_ref=s16.at[p, there, :, pl.ds(*lanes)], dst_ref=r2.at[p, r - 1, :, pl.ds(*lanes)], send_sem=chip_send.at[p, r - 1],
            recv_sem=chip_recv.at[p, r - 1], device_id=(z, there * 2 + core), device_id_type=MESH,
        )

    def core_sum(p):
        core_copy(p).wait_recv()
        both = d32[p, core] + r1[p].astype(F32)
        both = both.reshape(chips, per, 2 * cin)
        s32[p] = both
        s16[p] = both.astype(BF16)
        for_lanes(p, lambda lanes: [chip_copy(p, r, lanes).start() for r in range(1, chips)] and None)

    def weight_part(p, cot_rows, at, count):
        one = first_tap + 2 * p
        patches = jnp.concatenate(pair_tiles(split(one), split(one + 1), at, count), axis=1)
        return jnp.dot(cot_rows, patches, preferred_element_type=F32).reshape(d32.shape[1:])

    early = max(pairs - 1, 1)
    cot_all = jnp.concatenate([cot_t[s] for s in range(tm)], axis=1)
    for p in range(early):
        d32[p] = weight_part(p, cot_all, 0, total)
    pass_on(tm - 2, 0)
    pass_on(tm - 2, 1)
    lay_out(tm - 2)
    last = tm - 1 - z
    for p in range(pairs):
        if p < early:
            @pl.when((z == 0) | (z == tm - 1))
            def _():
                d32[p] = d32[p] + weight_part(p, cot_t[last], last * frames, frames)
        else:
            cot_all = jnp.concatenate([cot_t[s] for s in range(tm)], axis=1)
            d32[p] = weight_part(p, cot_all, 0, total)

        if fused:
            d16[p] = d32[p, 1 - core].astype(BF16)
            core_copy(p).start()
            if p > 0:
                core_sum(p - 1)
        else:
            gw_ref[:, p * 2 * cin : (p + 1) * 2 * cin] = d32[p].reshape(cout, 2 * cin)
    act_grad = act_grad + grad_range(24, 27)
    if fused:
        core_sum(pairs - 1)
    act_grad = act_grad + grad_range(0, 18)
    d_normed = act_grad * (sig * (1.0 + normed * (1.0 - sig))) * gain
    along = jnp.sum(d_normed * video, axis=1, keepdims=True) / cin
    vgrad_ref[...] = (inv * d_normed - video * (inv * inv * inv * along)).astype(BF16)

    if fused:
        scale = 1.0 / math.sqrt(dp * total * pixels)
        sums = []
        for p in range(pairs):
            own = s32[p, chip]
            for_lanes(p, lambda lanes: [chip_copy(p, r, lanes).wait_recv() for r in range(1, chips)] and None)
            for r in range(1, chips):
                own = own + r2[p, r - 1].astype(F32)
            sums.append(own * scale)
        wide = jnp.concatenate(sums, axis=1)
        wide = pltpu.roll(wide, pairs * 2 * cin - skip, axis=1)
        gw_ref[...] = wide[:, :slab]
        for p in range(pairs):
            core_copy(p).wait_send()
            for_lanes(p, lambda lanes: [chip_copy(p, r, lanes).wait_send() for r in range(1, chips)] and None)

    for step in range(tm - 1):
        @pl.when((z < tm - 1) & (z - step >= 0))
        def _():
            for h in range(2):
                to_right(step, z - step, h).wait_send()

        @pl.when((z > 0) & (z + step <= tm - 1))
        def _():
            for h in range(2):
                to_left(step, z + step, h).wait_send()


def emit(*refs):
    count = len(refs) // 2
    sems = refs[-1]
    copies = [pltpu.make_async_copy(refs[n], refs[count + n], sems.at[n]) for n in range(count)]
    for copy in copies:
        copy.start()
    for copy in copies:
        copy.wait()


def shards(sizes, clip_video, clip_ids, norm_gain, conv_weight, out_cotangent):
    tm, dp = sizes
    unused, frames, height, width, cin = clip_video.shape
    krows, cout = conv_weight.shape
    rows = frames * height * width
    total = tm * frames
    slab = krows // tm
    per = cout // dp
    spans = [-(-(z * slab % cin + slab) // cin) for z in range(tm)]
    pairs = (max(spans) + 1) // 2
    fused = per % 16 == 0
    chips = dp // 2
    chunks = cout // 128
    wide = 2 * pairs * cin
    gw_shape = (per, slab) if fused else (cout, wide)
    cfg = (tm, dp, frames, height, width, cin, cout, slab, pairs, fused)
    side = (pairs, 2, cout // 2, 2 * cin)
    one_side = (pairs, cout // 2, 2 * cin) if fused else (1, 16, 128)
    ends = (pairs, chips, per, 2 * cin) if fused else (1, 1, 16, 128)
    vmem = pl.BlockSpec(memory_space=pltpu.VMEM)
    hbm = pltpu.HBM
    pinned = [
        pltpu.with_memory_space_constraint(x, hbm)
        for x in (
            clip_video.reshape(rows, cin),
            norm_gain.reshape(1, cin),
            conv_weight,
            out_cotangent.reshape(rows, cout),
            clip_ids,
        )
    ]
    conv, vgrad, gw = pl.pallas_call(
        functools.partial(kernel, cfg),
        out_shape=(
            jax.ShapeDtypeStruct((rows, cout), BF16),
            jax.ShapeDtypeStruct((rows, cin), BF16),
            jax.ShapeDtypeStruct(gw_shape, F32),
        ),
        in_specs=[vmem, pl.BlockSpec(memory_space=pltpu.SMEM), vmem, pl.BlockSpec(memory_space=pl.ANY), vmem],
        out_specs=(vmem, vmem, vmem),
        scratch_shapes=[
            pltpu.VMEM((krows, cout), BF16),
            pltpu.VMEM((tm, (chunks + 1) * rows + rows // 2, 128), BF16),
            pltpu.VMEM((2, 3, total + 3, height + 2, width, 256), BF16),
            pltpu.VMEM((3, 2 * frames, height + 2, width, cout), BF16),
            pltpu.VMEM((4, total + 2, height * width, 128), BF16),
            pltpu.VMEM((tm, cout, rows), BF16),
            pltpu.VMEM(side, F32),
            pltpu.VMEM(one_side, BF16),
            pltpu.VMEM(one_side, BF16),
            pltpu.VMEM(ends, BF16),
            pltpu.VMEM(ends, F32),
            pltpu.VMEM(ends, BF16),
            pltpu.SemaphoreType.DMA,
            pltpu.SemaphoreType.DMA((tm, 2)),
            pltpu.SemaphoreType.DMA((tm, 2)),
            pltpu.SemaphoreType.DMA((tm, 2)),
            pltpu.SemaphoreType.DMA((tm, 2)),
            pltpu.SemaphoreType.DMA((pairs,)),
            pltpu.SemaphoreType.DMA((pairs,)),
            pltpu.SemaphoreType.DMA((pairs, chips)),
            pltpu.SemaphoreType.DMA((pairs, chips)),
        ],
        compiler_params=pltpu.CompilerParams(
            collective_id=0, has_side_effects=True, vmem_limit_bytes=40 * 1024 * 1024
        ),
    )(
        pinned[0],
        pinned[4],
        *pinned[1:4],
    )
    results = (conv, vgrad, gw)
    conv, vgrad, gw = pl.pallas_call(
        emit,
        out_shape=tuple(jax.ShapeDtypeStruct(x.shape, x.dtype) for x in results),
        in_specs=[pl.BlockSpec(memory_space=pl.ANY)] * 3,
        out_specs=(pl.BlockSpec(memory_space=pl.ANY),) * 3,
        scratch_shapes=[pltpu.SemaphoreType.DMA((3,))],
        compiler_params=pltpu.CompilerParams(vmem_limit_bytes=1024 * 1024),
    )(*results)
    if fused:
        grad_weight = gw.T
    else:
        scale = 1.0 / math.sqrt(dp * total * height * width)
        mine = lax.psum_scatter(gw * scale, "dp", scatter_dimension=0, tiled=True)
        z = lax.axis_index("tm")
        grad_weight = lax.dynamic_slice_in_dim(mine, z * slab % cin, slab, 1).T
    return (
        conv.reshape(1, frames, height, width, cout),
        vgrad.reshape(1, frames, height, width, cin),
        grad_weight,
    )


def solution(mesh):
    in_specs = (
        P("dp", "tm", None, None, None),
        P("dp", None),
        P(),
        P(),
        P("dp", "tm", None, None, None),
    )
    out_specs = (P("dp", "tm", None, None, None), P("dp", "tm", None, None, None), P("tm", "dp"))
    sizes = (mesh.shape["tm"], mesh.shape["dp"])
    return jax.shard_map(
        functools.partial(shards, sizes), mesh=mesh, in_specs=in_specs, out_specs=out_specs, check_vma=False
    )
```
